128 devices in a mesh: sx: 8 (over x, z_lo), sy: 16 (over y, z_hi, core).
Axes of the slice: x: 4, y: 4, z: 4 (z_hi: 2, z_lo: 2; z = z_hi * 2 + z_lo), core: 2. Of those that a mesh axis runs over, the one named last changes fastest.
Arguments:
- signal: bfloat16 [8, 16, 1024, 512], P('sx', 'sy'), may hold values from -6 to 6
- box_phase: float32 [13, 8, 16, 256], P(None, 'sx', 'sy'), may hold values from -3.140625 to 3.140625
- node_phase: float32 [13, 1024, 256], replicated, may hold values from -3.140625 to 3.140625
- local_interp: bfloat16 [2, 2, 2, 256, 256], replicated, may hold values from -0.1875 to 0.1875
- across_x: bfloat16 [2, 2, 2, 256, 256], replicated, may hold values from -0.1875 to 0.1875
- across_y: bfloat16 [2, 2, 2, 256, 256], replicated, may hold values from -0.1875 to 0.1875
Outputs:
- spectrum: bfloat16 [8, 16, 1024, 512], P('sx', 'sy')
The draws below stay inside these ranges and needn't reach their ends.
All inputs are finite; a program needn't handle non-finite values.
Results may differ from the reference program's by a relative error of at most 0.04.
Values may be sent and summed in bfloat16 or wider, within the bound.
No kernel may reach another device: no remote copies, remote signals or barrier semaphores. Data moves between devices by JAX's collectives and lax.ppermute only.
A program may use at most 128 MiB of HBM per device.

```python
import jax
import jax.numpy as jnp

M = 256
K = 1024
PRE_LEVELS = 3
POST_LEVELS = 3
BITS_X = 3
BITS_Y = 4
LEVELS = 13
NBX = 8
NBY = 16


def level_of(own_key, shape, split, smallest, largest):
    def one(dim, shards_of):
        draws = jax.random.uniform(jax.random.fold_in(jax.random.fold_in(own_key, 6), dim), (shards_of,), jnp.float32, smallest / len(split), largest / len(split))
        return jnp.repeat(jnp.exp(draws), shape[dim] // shards_of).reshape((-1,) + (1,) * (len(shape) - dim - 1))

    gain = one(*split[0])
    for cut in split[1:]:
        gain = gain * one(*cut)
    return gain


def noise(key, dims, deviation, limit, pieces=(), dtype=jnp.bfloat16):
    entries = jax.random.normal(key, dims, jnp.float32) * deviation
    if len(pieces) > 0:
        entries = level_of(key, dims, pieces, -0.22, 0.18) * entries
    return jnp.clip(entries, min=-limit, max=limit).astype(dtype)


def setup_inputs(seed: int = 0) -> dict:
    keys = jax.random.split(jax.random.key(seed), 7)
    return {
        "signal": noise(keys[0], (NBX, NBY, K, 2 * M), 1.0, 6.0, ((0, 8), (1, 16))),
        "box_phase": jnp.clip(jax.random.uniform(keys[1], (LEVELS, NBX, NBY, M), jnp.float32, -3.140625, 3.140625), -3.140625, 3.140625),
        "node_phase": jnp.clip(jax.random.uniform(keys[2], (LEVELS, K, M), jnp.float32, -3.140625, 3.140625), -3.140625, 3.140625),
        "local_interp": noise(keys[3], (2, 2, 2, M, M), (4 * M) ** -0.5, 0.1875),
        "across_x": noise(keys[4], (2, 2, 2, M, M), (4 * M) ** -0.5, 0.1875),
        "across_y": noise(keys[5], (2, 2, 2, M, M), (4 * M) ** -0.5, 0.1875),
    }


def rotate(current, angles):
    values = current.astype(jnp.float32)
    nodes = angles.shape[-1]
    real_part = values[..., :nodes]
    imag_part = values[..., nodes:]
    cosine = jnp.cos(angles)
    sine_part = jnp.sin(angles)
    joined = jnp.concatenate([real_part * cosine - imag_part * sine_part, real_part * sine_part + imag_part * cosine], axis=-1)
    return joined.astype(jnp.bfloat16)


def complex_block(interp, child, source):
    top_row = jnp.concatenate([interp[child, source, 0], interp[child, source, 1]], axis=1)
    low_row = jnp.concatenate([-interp[child, source, 1], interp[child, source, 0]], axis=1)
    return jnp.concatenate([top_row, low_row], axis=0)


def combined_matrix(interp):
    rows = []
    for source in range(2):
        rows.append(jnp.concatenate([complex_block(interp, 0, source), complex_block(interp, 1, source)], axis=1))
    return jnp.concatenate(rows, axis=0)


def pair_level(rotated, position, bit_pos, combined):
    shape = rotated.shape
    split_shape = shape[:position] + (shape[position] >> (bit_pos + 1), 2, 1 << bit_pos) + shape[position + 1:]
    moved = jnp.moveaxis(rotated.reshape(split_shape), position + 1, -2)
    leading = moved.shape[:-2]
    flat_rows = moved.reshape(-1, 2 * shape[-1])
    product = jnp.dot(flat_rows, combined, preferred_element_type=jnp.float32)
    restored = jnp.moveaxis(product.reshape(leading + (2, shape[-1])), -2, position + 1)
    return restored.reshape(shape).astype(jnp.bfloat16)


def build_plan():
    plan = []
    for bit_pos in range(PRE_LEVELS):
        plan.append((2, bit_pos, "local"))
    for step_pos in range(max(BITS_X, BITS_Y)):
        if step_pos < BITS_X:
            plan.append((0, step_pos, "first"))
        if step_pos < BITS_Y:
            plan.append((1, step_pos, "second"))
    for bit_pos in range(POST_LEVELS):
        plan.append((2, PRE_LEVELS + bit_pos, "local"))
    return plan


def reference(signal, box_phase, node_phase, local_interp, across_x, across_y):
    matrices = {"local": combined_matrix(local_interp), "first": combined_matrix(across_x), "second": combined_matrix(across_y)}
    current = signal
    for level, entry in enumerate(build_plan()):
        position, bit_pos, matrix_key = entry
        angles = box_phase[level][:, :, None, :] + node_phase[level][None, None]
        rotated = rotate(current, angles)
        current = pair_level(rotated, position, bit_pos, matrices[matrix_key])
    return current
```

```python
import functools

import jax
import jax.numpy as jnp
from jax import lax
from jax.experimental import pallas as pl
from jax.experimental.pallas import tpu as pltpu
from jax.sharding import PartitionSpec as P

AXES = ("sx", "sy")
ROWS = 1024
NODES = 256
WIDTH = 512
BOXES = 128
SLAB = 8
CHUNK = 64
INNER = 10
BOX_BITS = (4, 0, 5, 1, 6, 2, 3)
WEIGHT_OF = (0, 0, 0, 1, 2, 1, 2, 1, 2, 2)

SIN = (9.99999996e-01, -1.66666580e-01, 8.33305063e-03, -1.98090465e-04, 2.60516562e-06)
COS = (9.99999953e-01, -4.99999051e-01, 4.16635791e-02, -1.38536671e-03, 2.31531671e-05)


def horner(coefficients, x):
    total = coefficients[-1] * x + coefficients[-2]
    for factor in coefficients[-3::-1]:
        total = total * x + factor
    return total


def cos_sin(angle):
    half = angle * 0.5
    square = half * half
    sine = half * horner(SIN, square)
    cosine = horner(COS, square)
    double = sine + sine
    return 1.0 - double * sine, double * cosine


def pair_ranges(bit, half, start, count):
    distance = SLAB << bit
    length = min(distance, count)
    return [
        ((r // distance) * 2 * distance + half * distance + r % distance, length)
        for r in range(start, start + count, length)
    ]


def load_ranges(ref, ranges, columns):
    parts = [ref[r : r + n, columns] for r, n in ranges]
    return parts[0] if len(parts) == 1 else jnp.concatenate(parts, axis=0)


RE = slice(0, NODES)
IM = slice(NODES, WIDTH)


def prep_kernel(box_ref, node_ref, local_ref, x_ref, y_ref, weight_ref, cos_ref, sin_ref):
    step = pl.program_id(0)
    box_cos, box_sin = cos_sin(box_ref[0])
    for k, interp in enumerate((local_ref, x_ref, y_ref)):

        @pl.when(step == k)
        def _():
            for child in range(2):
                for source in range(2):
                    r, c = source * WIDTH, child * WIDTH
                    real, imag = interp[child, source, 0], interp[child, source, 1]
                    weight_ref[0, r : r + NODES, c : c + NODES] = real
                    weight_ref[0, r : r + NODES, c + NODES : c + WIDTH] = imag
                    weight_ref[0, r + NODES : r + WIDTH, c : c + NODES] = -imag
                    weight_ref[0, r + NODES : r + WIDTH, c + NODES : c + WIDTH] = real
            for half in range(2):
                for start in range(0, ROWS // 2, CHUNK):
                    angles = load_ranges(
                        node_ref.at[0], pair_ranges(k, half, start, CHUNK), slice(None)
                    )
                    node_cos, node_sin = cos_sin(angles)
                    rows = slice(half * (ROWS // 2) + start, half * (ROWS // 2) + start + CHUNK)
                    cos_ref[0, rows, :] = (node_cos * box_cos - node_sin * box_sin).astype(
                        jnp.bfloat16
                    )
                    sin_ref[0, rows, :] = (node_sin * box_cos + node_cos * box_sin).astype(
                        jnp.bfloat16
                    )


def prep(box_phase, node_phase, interps):
    whole = pl.BlockSpec((2, 2, 2, NODES, NODES), lambda i: (0, 0, 0, 0, 0))
    table = pl.BlockSpec((1, ROWS, NODES), lambda i: (i, 0, 0))
    return pl.pallas_call(
        prep_kernel,
        grid=(3,),
        in_specs=[
            pl.BlockSpec((1, 1, NODES), lambda i: (i, 0, 0)),
            pl.BlockSpec((1, ROWS, NODES), lambda i: (INNER + i, 0, 0)),
            whole,
            whole,
            whole,
        ],
        out_specs=[pl.BlockSpec((1, 2 * WIDTH, 2 * WIDTH), lambda i: (i, 0, 0)), table, table],
        out_shape=[
            jax.ShapeDtypeStruct((3, 2 * WIDTH, 2 * WIDTH), jnp.bfloat16),
            jax.ShapeDtypeStruct((3, ROWS, NODES), jnp.bfloat16),
            jax.ShapeDtypeStruct((3, ROWS, NODES), jnp.bfloat16),
        ],
        compiler_params=pltpu.CompilerParams(vmem_limit_bytes=32 << 20),
        cost_estimate=pl.CostEstimate(flops=60_000_000, bytes_accessed=15 << 20, transcendentals=0),
        name="prep",
    )(box_phase, node_phase, *interps)


def table_kernel(me_ref, bit_ref, near_ref, far_ref, node_ref, cos_ref, sin_ref, box_cos, box_sin):
    level = pl.program_id(0)
    me = me_ref[0]

    def place(p, carry):
        offset = (
            32 * (p & 3) + 4 * ((p >> 2) & 3) + 16 * ((p >> 4) & 1) + 2 * ((p >> 5) & 1)
        )
        box = me ^ offset
        row = p * INNER + level
        box_cos[pl.ds(box, 1), :] = near_ref[pl.ds(row, 1), :]
        box_cos[pl.ds(box ^ 1, 1), :] = far_ref[pl.ds(row, 1), :]
        return carry

    lax.fori_loop(0, BOXES // 2, place, 0, unroll=8)
    cosines, sines = cos_sin(box_cos[...])
    box_cos[...] = cosines
    box_sin[...] = sines
    node_cos, node_sin = cos_sin(node_ref[0])

    for k in range(3):

        @pl.when(level == k)
        def _():
            order = [w for w in range(SLAB) if not w >> k & 1] + [
                w for w in range(SLAB) if w >> k & 1
            ]
            for i, w in enumerate(order):
                rows = slice(i * BOXES, (i + 1) * BOXES)
                c, s = node_cos[w : w + 1], node_sin[w : w + 1]
                cos_ref[0, rows, :] = (box_cos[...] * c - box_sin[...] * s).astype(jnp.bfloat16)
                sin_ref[0, rows, :] = (box_sin[...] * c + box_cos[...] * s).astype(jnp.bfloat16)

    @pl.when(level >= 3)
    def _():
        bit = bit_ref[level]

        def fill(i, carry):
            cos_rows, sin_rows = [], []
            for j in range(2):
                q = 2 * i + j
                r = q & (BOXES // 2 - 1)
                half = q >> 6
                low = lax.shift_left(jnp.int32(1), bit) - 1
                box = ((r & ~low) << 1) | lax.shift_left(half, bit) | (r & low)
                c, s = box_cos[pl.ds(box, 1), :], box_sin[pl.ds(box, 1), :]
                cos_rows.append(c * node_cos - s * node_sin)
                sin_rows.append(s * node_cos + c * node_sin)
            rows = pl.ds(pl.multiple_of(i * 2 * SLAB, 2 * SLAB), 2 * SLAB)
            cos_ref[0, rows, :] = jnp.concatenate(cos_rows, axis=0).astype(jnp.bfloat16)
            sin_ref[0, rows, :] = jnp.concatenate(sin_rows, axis=0).astype(jnp.bfloat16)
            return carry

        lax.fori_loop(0, BOXES // 2, fill, 0, unroll=8)


def tables(me, near, far, node_phase):
    bits = jnp.asarray((0, 0, 0) + BOX_BITS, jnp.int32)
    half = pl.BlockSpec((BOXES // 2 * INNER, NODES), lambda i, me, bits: (0, 0))
    table = pl.BlockSpec((1, ROWS, NODES), lambda i, me, bits: (i, 0, 0))
    shape = jax.ShapeDtypeStruct((INNER, ROWS, NODES), jnp.bfloat16)
    return pl.pallas_call(
        table_kernel,
        grid_spec=pltpu.PrefetchScalarGridSpec(
            num_scalar_prefetch=2,
            grid=(INNER,),
            in_specs=[half, half, pl.BlockSpec((1, SLAB, NODES), lambda i, me, bits: (i, me[0], 0))],
            out_specs=[table, table],
            scratch_shapes=[pltpu.VMEM((BOXES, NODES), jnp.float32)] * 2,
        ),
        out_shape=[shape, shape],
        compiler_params=pltpu.CompilerParams(vmem_limit_bytes=32 << 20),
        cost_estimate=pl.CostEstimate(flops=60_000_000, bytes_accessed=13 << 20, transcendentals=0),
        name="tables",
    )(me, bits, near, far, node_phase)


def rotate_into(mixed, rows, half, values_re, values_im, cosine, sine):
    c, s = cosine.astype(jnp.float32), sine.astype(jnp.float32)
    left = half * WIDTH
    mixed[rows, left : left + NODES] = (values_re * c - values_im * s).astype(jnp.bfloat16)
    mixed[rows, left + NODES : left + WIDTH] = (values_re * s + values_im * c).astype(jnp.bfloat16)


def paired_level(bit, source, target, cos_ref, sin_ref, mixed, weight):
    for half in range(2):
        for start in range(0, ROWS // 2, CHUNK):
            ranges = pair_ranges(bit, half, start, CHUNK)
            table = slice(half * (ROWS // 2) + start, half * (ROWS // 2) + start + CHUNK)
            rotate_into(
                mixed,
                slice(start, start + CHUNK),
                half,
                load_ranges(source, ranges, RE),
                load_ranges(source, ranges, IM),
                cos_ref[0, table, :],
                sin_ref[0, table, :],
            )
    for part in range(4):
        half, columns = part >> 1, (RE, IM)[part & 1]
        product = jnp.dot(
            mixed[...],
            weight[:, part * NODES : (part + 1) * NODES],
            preferred_element_type=jnp.float32,
        )
        at = 0
        for r, n in pair_ranges(bit, half, 0, ROWS // 2):
            target[r : r + n, columns] = product[at : at + n].astype(target.dtype)
            at += n


def row_level(bit, strided, slabs, cos_ref, sin_ref, mixed, weight):
    order = [[w for w in range(SLAB) if (w >> bit & 1) == half] for half in range(2)]
    for half in range(2):
        for i, w in enumerate(order[half]):
            rows = slice(i * BOXES, (i + 1) * BOXES)
            table = slice(half * (ROWS // 2) + i * BOXES, half * (ROWS // 2) + (i + 1) * BOXES)
            if bit == 0:
                parts = [strided[j, pl.ds(w, BOXES, stride=SLAB), :] for j in range(4)]
                re, im = jnp.concatenate(parts[:2], axis=1), jnp.concatenate(parts[2:], axis=1)
            else:
                re = slabs[w * BOXES : (w + 1) * BOXES, RE]
                im = slabs[w * BOXES : (w + 1) * BOXES, IM]
            rotate_into(mixed, rows, half, re, im, cos_ref[0, table, :], sin_ref[0, table, :])
    for part in range(4):
        half = part >> 1
        product = jnp.dot(
            mixed[...],
            weight[:, part * NODES : (part + 1) * NODES],
            preferred_element_type=jnp.float32,
        )
        for i, w in enumerate(order[half]):
            piece = product[i * BOXES : (i + 1) * BOXES]
            if bit == 2:
                for j in range(2):
                    strided[2 * (part & 1) + j, pl.ds(w, BOXES, stride=SLAB), :] = piece[
                        :, j * 128 : (j + 1) * 128
                    ]
            else:
                slabs[w * BOXES : (w + 1) * BOXES, (RE, IM)[part & 1]] = piece


class Strips:
    def __init__(self, ref):
        self.ref = ref

    def __getitem__(self, index):
        rows, columns = index
        first = columns.start // 128
        return jnp.concatenate([self.ref[first, rows, :], self.ref[first + 1, rows, :]], axis=1)


def inner_kernel(
    data_ref, cos_ref, sin_ref, weight_hbm, out_ref, strided, slabs, current, mixed, weights, sems
):
    level = pl.program_id(0)
    copies = [pltpu.make_async_copy(weight_hbm.at[k], weights.at[k], sems.at[k]) for k in range(3)]

    @pl.when(level == 0)
    def _():
        for copy in copies:
            copy.start()
        for j in range(4):
            strided[j] = data_ref[:, j * 128 : (j + 1) * 128].astype(jnp.float32)
        copies[0].wait()
        row_level(0, strided, slabs, cos_ref, sin_ref, mixed, weights.at[0])

    for k in (1, 2):

        @pl.when(level == k)
        def _():
            row_level(k, strided, slabs, cos_ref, sin_ref, mixed, weights.at[0])

    for k, bit in enumerate(BOX_BITS):

        @pl.when(level == 3 + k)
        def _():
            if k < 2:
                copies[1 + k].wait()
            source = Strips(strided) if k == 0 else current
            target = out_ref if k == len(BOX_BITS) - 1 else current
            weight = weights.at[WEIGHT_OF[3 + k]]
            paired_level(bit, source, target, cos_ref, sin_ref, mixed, weight)


def inner_levels(data, cosines, sines, weights):
    whole = pl.BlockSpec((ROWS, WIDTH), lambda i: (0, 0))
    table = pl.BlockSpec((1, ROWS, NODES), lambda i: (i, 0, 0))
    return pl.pallas_call(
        inner_kernel,
        grid=(INNER,),
        in_specs=[whole, table, table, pl.BlockSpec(memory_space=pl.ANY)],
        out_specs=whole,
        out_shape=jax.ShapeDtypeStruct((ROWS, WIDTH), jnp.bfloat16),
        scratch_shapes=[
            pltpu.VMEM((4, ROWS, 128), jnp.float32),
            pltpu.VMEM((ROWS, WIDTH), jnp.float32),
            pltpu.VMEM((ROWS, WIDTH), jnp.float32),
            pltpu.VMEM((ROWS // 2, 2 * WIDTH), jnp.bfloat16),
            pltpu.VMEM((3, 2 * WIDTH, 2 * WIDTH), jnp.bfloat16),
            pltpu.SemaphoreType.DMA((3,)),
        ],
        compiler_params=pltpu.CompilerParams(vmem_limit_bytes=48 << 20),
        cost_estimate=pl.CostEstimate(
            flops=INNER << 30, bytes_accessed=18 << 20, transcendentals=0
        ),
        name="inner",
    )(data, cosines, sines, weights)


def outer_kernel(data_ref, cos_ref, sin_ref, weight_ref, out_ref, current, mixed):
    level = pl.program_id(0)
    weight = weight_ref.at[0]

    @pl.when(level == 0)
    def _():
        current[...] = data_ref[...].astype(jnp.float32)

    for k in range(3):

        @pl.when(level == k)
        def _():
            target = out_ref if k == 2 else current
            paired_level(k, current, target, cos_ref, sin_ref, mixed, weight)


def outer_levels(data, cosines, sines, weights):
    whole = pl.BlockSpec((ROWS, WIDTH), lambda i: (0, 0))
    table = pl.BlockSpec((1, ROWS, NODES), lambda i: (i, 0, 0))
    return pl.pallas_call(
        outer_kernel,
        grid=(3,),
        in_specs=[whole, table, table, pl.BlockSpec((1, 2 * WIDTH, 2 * WIDTH), lambda i: (0, 0, 0))],
        out_specs=whole,
        out_shape=jax.ShapeDtypeStruct((ROWS, WIDTH), jnp.bfloat16),
        scratch_shapes=[
            pltpu.VMEM((ROWS, WIDTH), jnp.float32),
            pltpu.VMEM((ROWS // 2, 2 * WIDTH), jnp.bfloat16),
        ],
        compiler_params=pltpu.CompilerParams(vmem_limit_bytes=48 << 20),
        cost_estimate=pl.CostEstimate(flops=3 << 30, bytes_accessed=8 << 20, transcendentals=0),
        name="outer",
    )(data, cosines, sines, weights)


def exchange(rows):
    return lax.all_to_all(rows, AXES, 0, 0, tiled=True)


def from_offset(block, offset):
    return lax.ppermute(block, AXES, [(i, i ^ offset) for i in range(BOXES)])


def on_device(signal, box_phase, node_phase, local_interp, across_x, across_y):
    me = (lax.axis_index("sx") * lax.axis_size("sy") + lax.axis_index("sy")).astype(jnp.int32)
    moved = exchange(signal[0, 0])
    near = box_phase[:INNER, 0, 0]
    for offsets in ((32, 64, 96), (4, 8, 12), (16, 2, 18)):
        near = jnp.concatenate([near] + [from_offset(near, m) for m in offsets], axis=0)
    far = from_offset(near, 1)
    weights, outer_cos, outer_sin = prep(
        box_phase[INNER:, 0], node_phase, (local_interp, across_x, across_y)
    )
    inner_cos, inner_sin = tables(me[None], near, far, node_phase)
    inner = inner_levels(moved, inner_cos, inner_sin, weights)
    back = exchange(inner)
    return outer_levels(back, outer_cos, outer_sin, weights)[None, None]


def solution(mesh):
    return jax.shard_map(
        on_device,
        mesh=mesh,
        in_specs=(P("sx", "sy", None, None), P(None, "sx", "sy", None), P(), P(), P(), P()),
        out_specs=P("sx", "sy", None, None),
        check_vma=False,
    )
```

```python
import functools

import jax
import jax.numpy as jnp
from jax import lax
from jax.experimental import pallas as pl
from jax.experimental.pallas import tpu as pltpu
from jax.sharding import PartitionSpec as P

AXES = ("sx", "sy")
ROWS = 1024
NODES = 256
WIDTH = 512
BOXES = 128
SLAB = 8
CHUNK = 64
FIRST = 3
INNER = 7
LAST = FIRST + INNER
BLOCK = 256
BOX_BITS = (4, 0, 5, 1, 6, 2, 3)
SECOND = (0, 1, 0, 1, 0, 1, 1)

SIN = (9.99999996e-01, -1.66666580e-01, 8.33305063e-03, -1.98090465e-04, 2.60516562e-06)
COS = (9.99999953e-01, -4.99999051e-01, 4.16635791e-02, -1.38536671e-03, 2.31531671e-05)


def horner(coefficients, x):
    total = coefficients[-1] * x + coefficients[-2]
    for factor in coefficients[-3::-1]:
        total = total * x + factor
    return total


def cos_sin(angle):
    half = angle * 0.5
    square = half * half
    sine = half * horner(SIN, square)
    cosine = horner(COS, square)
    double = sine + sine
    return 1.0 - double * sine, double * cosine


def pair_ranges(bit, half, start, count):
    distance = SLAB << bit
    length = min(distance, count)
    return [
        ((r // distance) * 2 * distance + half * distance + r % distance, length)
        for r in range(start, start + count, length)
    ]


def load_ranges(ref, ranges, columns):
    parts = [ref[r : r + n, columns] for r, n in ranges]
    return parts[0] if len(parts) == 1 else jnp.concatenate(parts, axis=0)


RE = slice(0, NODES)
IM = slice(NODES, WIDTH)


VMEM = pl.BlockSpec(memory_space=pltpu.VMEM)


def fill_weight(weight, interp):
    for child in range(2):
        for source in range(2):
            r, c = source * WIDTH, child * WIDTH
            real, imag = interp[child, source, 0], interp[child, source, 1]
            weight[r : r + NODES, c : c + NODES] = real
            weight[r : r + NODES, c + NODES : c + WIDTH] = imag
            weight[r + NODES : r + WIDTH, c : c + NODES] = -imag
            weight[r + NODES : r + WIDTH, c + NODES : c + WIDTH] = real


def rotate_into(mixed, rows, half, re, im, c, s):
    left = half * WIDTH
    mixed[rows, left : left + NODES] = (re * c - im * s).astype(jnp.bfloat16)
    mixed[rows, left + NODES : left + WIDTH] = (re * s + im * c).astype(jnp.bfloat16)


def row_level(bit, load, store, node_refs, box, mixed, weight):
    box_cos, box_sin = box
    order = [[w for w in range(SLAB) if (w >> bit & 1) == half] for half in range(2)]
    for first in range(0, SLAB // 2, BLOCK // BOXES):
        slots = range(first, first + BLOCK // BOXES)
        for half in range(2):
            for i in slots:
                w = order[half][i]
                angles = [ref[0, pl.ds(w, BOXES, stride=SLAB), :] for ref in node_refs]
                node_cos, node_sin = cos_sin(jnp.concatenate(angles, axis=1))
                rotate_into(
                    mixed,
                    slice(i * BOXES, (i + 1) * BOXES),
                    half,
                    load(w, RE),
                    load(w, IM),
                    node_cos * box_cos - node_sin * box_sin,
                    node_sin * box_cos + node_cos * box_sin,
                )
        rows = slice(first * BOXES, first * BOXES + BLOCK)
        for part in range(4):
            product = jnp.dot(
                mixed[rows],
                weight[:, part * NODES : (part + 1) * NODES],
                preferred_element_type=jnp.float32,
            )
            for at, i in enumerate(slots):
                piece = product[at * BOXES : (at + 1) * BOXES]
                store(order[part >> 1][i], (RE, IM)[part & 1], piece)


def start_kernel(data_ref, box_ref, left, right, interp_ref, out_ref, weight, strided, mixed):
    fill_weight(weight, interp_ref)
    for j in range(4):
        strided[j] = data_ref[:, j * 128 : (j + 1) * 128].astype(jnp.float32)

    def load(w, columns):
        first = columns.start // 128
        parts = [strided[first + j, pl.ds(w, BOXES, stride=SLAB), :] for j in range(2)]
        return jnp.concatenate(parts, axis=1)

    def store(w, columns, piece):
        out_ref[w * BOXES : (w + 1) * BOXES, columns] = piece.astype(jnp.bfloat16)

    row_level(0, load, store, (left, right), cos_sin(box_ref[0]), mixed, weight)


def node_strips(level):
    return [pl.BlockSpec((1, ROWS, 128), functools.partial(lambda j, i: (level, 0, j), j)) for j in range(2)]


def whole(*shape):
    return pl.BlockSpec(shape, lambda i: (0,) * len(shape))


def start_level(data, box_phase, node_phase, interp):
    return pl.pallas_call(
        start_kernel,
        grid=(1,),
        in_specs=[
            whole(ROWS, WIDTH),
            whole(1, 1, NODES),
            *node_strips(0),
            whole(2, 2, 2, NODES, NODES),
        ],
        out_specs=[VMEM, VMEM],
        out_shape=[
            jax.ShapeDtypeStruct((ROWS, WIDTH), jnp.bfloat16),
            jax.ShapeDtypeStruct((2 * WIDTH, 2 * WIDTH), jnp.bfloat16),
        ],
        scratch_shapes=[
            pltpu.VMEM((4, ROWS, 128), jnp.float32),
            pltpu.VMEM((ROWS // 2, 2 * WIDTH), jnp.bfloat16),
        ],
        compiler_params=pltpu.CompilerParams(vmem_limit_bytes=24 << 20),
        cost_estimate=pl.CostEstimate(flops=1 << 30, bytes_accessed=5 << 20, transcendentals=0),
        name="level0",
    )(data, box_phase, node_phase, node_phase, interp)


def pair_kernel(
    data_ref, box_ref, left1, right1, left2, right2, weight, out_ref, strided, slabs, mixed
):
    def load_first(w, columns):
        return data_ref[w * BOXES : (w + 1) * BOXES, columns].astype(jnp.float32)

    def load(w, columns):
        return slabs[w * BOXES : (w + 1) * BOXES, columns]

    def store(w, columns, piece):
        slabs[w * BOXES : (w + 1) * BOXES, columns] = piece

    def store_last(w, columns, piece):
        first = columns.start // 128
        for j in range(2):
            strided[first + j, pl.ds(w, BOXES, stride=SLAB), :] = piece[:, j * 128 : (j + 1) * 128]

    row_level(1, load_first, store, (left1, right1), cos_sin(box_ref[0]), mixed, weight)
    row_level(2, load, store_last, (left2, right2), cos_sin(box_ref[1]), mixed, weight)
    for j in range(4):
        out_ref[:, j * 128 : (j + 1) * 128] = strided[j].astype(jnp.bfloat16)


def pair_levels(data, box_phase, node_phase, weight):
    return pl.pallas_call(
        pair_kernel,
        grid=(1,),
        in_specs=[VMEM, whole(2, 1, NODES), *node_strips(1), *node_strips(2), VMEM],
        out_specs=VMEM,
        out_shape=jax.ShapeDtypeStruct((ROWS, WIDTH), jnp.bfloat16),
        scratch_shapes=[
            pltpu.VMEM((4, ROWS, 128), jnp.float32),
            pltpu.VMEM((ROWS, WIDTH), jnp.float32),
            pltpu.VMEM((ROWS // 2, 2 * WIDTH), jnp.bfloat16),
        ],
        compiler_params=pltpu.CompilerParams(vmem_limit_bytes=24 << 20),
        cost_estimate=pl.CostEstimate(flops=2 << 30, bytes_accessed=5 << 20, transcendentals=0),
        name="levels12",
    )(data, box_phase, *[node_phase] * 4, weight)


def prep_kernel(box_ref, node_ref, x_ref, y_ref, x_weight, y_weight, cos_ref, sin_ref):
    step = pl.program_id(0)
    box_cos, box_sin = cos_sin(box_ref[0])
    for k in range(3):

        @pl.when(step == k)
        def _():
            if k == 0:
                fill_weight(x_weight, x_ref)
            if k == 1:
                fill_weight(y_weight, y_ref)
            for half in range(2):
                for start in range(0, ROWS // 2, CHUNK):
                    angles = load_ranges(
                        node_ref.at[0], pair_ranges(k, half, start, CHUNK), slice(None)
                    )
                    node_cos, node_sin = cos_sin(angles)
                    at = half * (ROWS // 2) + start
                    cosine = node_cos * box_cos - node_sin * box_sin
                    sine = node_sin * box_cos + node_cos * box_sin
                    cos_ref[k, at : at + CHUNK, :] = cosine.astype(jnp.bfloat16)
                    sin_ref[k, at : at + CHUNK, :] = sine.astype(jnp.bfloat16)


def prep(box_phase, node_phase, across_x, across_y):
    weight = jax.ShapeDtypeStruct((2 * WIDTH, 2 * WIDTH), jnp.bfloat16)
    table = jax.ShapeDtypeStruct((3, ROWS, NODES), jnp.bfloat16)
    return pl.pallas_call(
        prep_kernel,
        grid=(3,),
        in_specs=[
            pl.BlockSpec((1, 1, NODES), lambda i: (i, 0, 0)),
            pl.BlockSpec((1, ROWS, NODES), lambda i: (LAST + i, 0, 0)),
            whole(2, 2, 2, NODES, NODES),
            whole(2, 2, 2, NODES, NODES),
        ],
        out_specs=[VMEM] * 4,
        out_shape=[weight, weight, table, table],
        compiler_params=pltpu.CompilerParams(vmem_limit_bytes=24 << 20),
        cost_estimate=pl.CostEstimate(flops=60_000_000, bytes_accessed=15 << 20, transcendentals=0),
        name="prep",
    )(box_phase, node_phase, across_x, across_y)


def table_kernel(me_ref, bit_ref, near_ref, far_ref, node_ref, cos_ref, sin_ref, box_cos, box_sin):
    step = pl.program_id(0)

    @pl.when(step == 0)
    def _():
        me = me_ref[0]

        def place(p, carry):
            offset = 32 * (p & 3) + 4 * ((p >> 2) & 3) + 16 * ((p >> 4) & 1) + 2 * ((p >> 5) & 1)
            rows = pl.ds(pl.multiple_of(p * SLAB, SLAB), SLAB)
            for box, ref in ((me ^ offset, near_ref), (me ^ offset ^ 1, far_ref)):
                c, s = cos_sin(ref[rows, :])
                to = pl.ds(pl.multiple_of(box * SLAB, SLAB), SLAB)
                box_cos[to, :] = c
                box_sin[to, :] = s
            return carry

        lax.fori_loop(0, BOXES // 2, place, 0, unroll=8)

    node_cos, node_sin = cos_sin(node_ref[0])
    bit = bit_ref[step]
    low = lax.shift_left(jnp.int32(1), bit) - 1

    def fill(i, carry):
        cos_rows, sin_rows = [], []
        for j in range(2):
            q = 2 * i + j
            r = q & (BOXES // 2 - 1)
            box = ((r & ~low) << 1) | lax.shift_left(q >> 6, bit) | (r & low)
            row = pl.ds(box * SLAB + step + 1, 1)
            c, s = box_cos[row, :], box_sin[row, :]
            cos_rows.append(c * node_cos - s * node_sin)
            sin_rows.append(s * node_cos + c * node_sin)
        rows = pl.ds(pl.multiple_of(i * 2 * SLAB, 2 * SLAB), 2 * SLAB)
        cos_ref[step, rows, :] = jnp.concatenate(cos_rows, axis=0).astype(jnp.bfloat16)
        sin_ref[step, rows, :] = jnp.concatenate(sin_rows, axis=0).astype(jnp.bfloat16)
        return carry

    lax.fori_loop(0, BOXES // 2, fill, 0, unroll=8)


def tables(me, near, far, node_phase):
    bits = jnp.asarray(BOX_BITS, jnp.int32)
    shape = jax.ShapeDtypeStruct((INNER, ROWS, NODES), jnp.bfloat16)
    return pl.pallas_call(
        table_kernel,
        grid_spec=pltpu.PrefetchScalarGridSpec(
            num_scalar_prefetch=2,
            grid=(INNER,),
            in_specs=[
                VMEM,
                VMEM,
                pl.BlockSpec((1, SLAB, NODES), lambda i, me, bits: (FIRST + i, me[0], 0)),
            ],
            out_specs=[VMEM, VMEM],
            scratch_shapes=[pltpu.VMEM((BOXES * SLAB, NODES), jnp.float32)] * 2,
        ),
        out_shape=[shape, shape],
        compiler_params=pltpu.CompilerParams(vmem_limit_bytes=24 << 20),
        cost_estimate=pl.CostEstimate(flops=60_000_000, bytes_accessed=9 << 20, transcendentals=0),
        name="tables",
    )(me, bits, near, far, node_phase)


def paired_level(bit, source, target, cosines, sines, mixed, weight):
    for first in range(0, ROWS // 2, BLOCK):
        for half in range(2):
            for start in range(first, first + BLOCK, CHUNK):
                ranges = pair_ranges(bit, half, start, CHUNK)
                at = half * (ROWS // 2) + start
                rotate_into(
                    mixed,
                    slice(start, start + CHUNK),
                    half,
                    load_ranges(source, ranges, RE).astype(jnp.float32),
                    load_ranges(source, ranges, IM).astype(jnp.float32),
                    cosines[at : at + CHUNK, :].astype(jnp.float32),
                    sines[at : at + CHUNK, :].astype(jnp.float32),
                )
        for part in range(4):
            product = jnp.dot(
                mixed[first : first + BLOCK],
                weight[:, part * NODES : (part + 1) * NODES],
                preferred_element_type=jnp.float32,
            )
            at = 0
            for r, n in pair_ranges(bit, part >> 1, first, BLOCK):
                target[r : r + n, (RE, IM)[part & 1]] = product[at : at + n].astype(target.dtype)
                at += n


def inner_kernel(data_ref, cos_ref, sin_ref, x_weight, y_weight, out_ref, current, mixed):
    current[...] = data_ref[...].astype(jnp.float32)
    for k, bit in enumerate(BOX_BITS):
        target = out_ref if k == INNER - 1 else current
        weight = y_weight if SECOND[k] else x_weight
        paired_level(bit, current, target, cos_ref.at[k], sin_ref.at[k], mixed, weight)


def outer_kernel(data_ref, cos_ref, sin_ref, weight, out_ref, current, mixed):
    current[...] = data_ref[...].astype(jnp.float32)
    for k in range(3):
        target = out_ref if k == 2 else current
        paired_level(k, current, target, cos_ref.at[k], sin_ref.at[k], mixed, weight)


def run_levels(kernel, count, *operands):
    return pl.pallas_call(
        kernel,
        in_specs=[VMEM] * len(operands),
        out_specs=VMEM,
        out_shape=jax.ShapeDtypeStruct((ROWS, WIDTH), jnp.bfloat16),
        scratch_shapes=[
            pltpu.VMEM((ROWS, WIDTH), jnp.float32),
            pltpu.VMEM((ROWS // 2, 2 * WIDTH), jnp.bfloat16),
        ],
        compiler_params=pltpu.CompilerParams(vmem_limit_bytes=24 << 20),
        cost_estimate=pl.CostEstimate(
            flops=count << 30, bytes_accessed=8 << 20, transcendentals=0
        ),
        name="levels" + str(count),
    )(*operands)


def exchange(rows):
    return lax.all_to_all(rows, AXES, 0, 0, tiled=True)


def from_offset(block, offset):
    return lax.ppermute(block, AXES, [(i, i ^ offset) for i in range(BOXES)])


def spread(block, offsets):
    return jnp.concatenate([block] + [from_offset(block, m) for m in offsets], axis=0)


def on_device(signal, box_phase, node_phase, local_interp, across_x, across_y):
    me = (lax.axis_index("sx") * lax.axis_size("sy") + lax.axis_index("sy")).astype(jnp.int32)
    own = box_phase[:, 0]
    near = spread(own[FIRST - 1 : LAST, 0], (32, 64, 96))
    current, local = start_level(signal[0, 0], own[:1], node_phase, local_interp)
    current, near = lax.optimization_barrier((current, near))
    near = spread(near, (4, 8, 12))
    current = pair_levels(current, own[1:FIRST], node_phase, local)
    current, near = lax.optimization_barrier((current, near))
    near = spread(near, (16, 2, 18))
    moved = exchange(current)
    far = from_offset(near, 1)
    x_weight, y_weight, outer_cos, outer_sin = prep(own[LAST:], node_phase, across_x, across_y)
    inner_cos, inner_sin = tables(me[None], near, far, node_phase)
    inner = run_levels(inner_kernel, INNER, moved, inner_cos, inner_sin, x_weight, y_weight)
    back = exchange(inner)
    return run_levels(outer_kernel, 3, back, outer_cos, outer_sin, local)[None, None]


def solution(mesh):
    return jax.shard_map(
        on_device,
        mesh=mesh,
        in_specs=(P("sx", "sy", None, None), P(None, "sx", "sy", None), P(), P(), P(), P()),
        out_specs=P("sx", "sy", None, None),
        check_vma=False,
    )
```

```python
import jax
import jax.numpy as jnp
from jax import lax
from jax.experimental import pallas as pl
from jax.experimental.pallas import tpu as pltpu
from jax.sharding import PartitionSpec as P

AXES = ("sx", "sy")
ROWS = 1024
NODES = 256
WIDTH = 512
BOXES = 128
SLAB = 8
CHUNK = 64
STRIP = 128
CODE = 38.0
MESSAGE = 48
DATA = 32
FIRST = 3
INNER = 7
LAST = FIRST + INNER
BLOCK = 256
BOX_BITS = (4, 0, 5, 1, 6, 2, 3)
SECOND = (0, 1, 0, 1, 0, 1, 1)

SIN = (9.99999996e-01, -1.66666580e-01, 8.33305063e-03, -1.98090465e-04, 2.60516562e-06)
COS = (9.99999953e-01, -4.99999051e-01, 4.16635791e-02, -1.38536671e-03, 2.31531671e-05)


def horner(coefficients, x):
    total = coefficients[-1] * x + coefficients[-2]
    for factor in coefficients[-3::-1]:
        total = total * x + factor
    return total


def cos_sin(angle):
    half = angle * 0.5
    square = half * half
    sine = half * horner(SIN, square)
    cosine = horner(COS, square)
    double = sine + sine
    return 1.0 - double * sine, double * cosine


def pair_ranges(bit, half, start, count):
    distance = SLAB << bit
    length = min(distance, count)
    return [
        ((r // distance) * 2 * distance + half * distance + r % distance, length)
        for r in range(start, start + count, length)
    ]


def load_ranges(ref, ranges, columns):
    parts = [ref[r : r + n, columns] for r, n in ranges]
    return parts[0] if len(parts) == 1 else jnp.concatenate(parts, axis=0)


RE = slice(0, NODES)
IM = slice(NODES, WIDTH)


VMEM = pl.BlockSpec(memory_space=pltpu.VMEM)
HBM = pl.BlockSpec(memory_space=pltpu.HBM)
DMA = pltpu.SemaphoreType.DMA


def fill_weight(weight, interp):
    for child in range(2):
        for source in range(2):
            r, c = source * WIDTH, child * WIDTH
            real, imag = interp[child, source, 0], interp[child, source, 1]
            weight[r : r + NODES, c : c + NODES] = real
            weight[r : r + NODES, c + NODES : c + WIDTH] = imag
            weight[r + NODES : r + WIDTH, c : c + NODES] = -imag
            weight[r + NODES : r + WIDTH, c + NODES : c + WIDTH] = real


def strip(j):
    return slice(j * STRIP, (j + 1) * STRIP)


def rotate_into(mixed, rows, half, re, im, c, s):
    left = half * WIDTH
    mixed[rows, left : left + NODES] = (re * c - im * s).astype(jnp.bfloat16)
    mixed[rows, left + NODES : left + WIDTH] = (re * s + im * c).astype(jnp.bfloat16)


def row_level(bit, load, store, nodes, box, mixed, weight):
    box_cos, box_sin = box
    order = [[w for w in range(SLAB) if (w >> bit & 1) == half] for half in range(2)]
    for first in range(0, SLAB // 2, BLOCK // BOXES):
        slots = range(first, first + BLOCK // BOXES)
        for half in range(2):
            for i in slots:
                w = order[half][i]
                angles = [nodes[bit, j, pl.ds(w, BOXES, stride=SLAB), :] for j in range(2)]
                node_cos, node_sin = cos_sin(jnp.concatenate(angles, axis=1))
                rotate_into(
                    mixed,
                    slice(i * BOXES, (i + 1) * BOXES),
                    half,
                    load(w, RE),
                    load(w, IM),
                    node_cos * box_cos - node_sin * box_sin,
                    node_sin * box_cos + node_cos * box_sin,
                )
        rows = slice(first * BOXES, first * BOXES + BLOCK)
        for part in range(4):
            product = jnp.dot(
                mixed[rows],
                weight[:, part * NODES : (part + 1) * NODES],
                preferred_element_type=jnp.float32,
            )
            for at, i in enumerate(slots):
                piece = product[at * BOXES : (at + 1) * BOXES]
                store(order[part >> 1][i], (RE, IM)[part & 1], piece)


def first_kernel(
    data_hbm, box_ref, node_hbm, interp_hbm, out_ref, weight,
    data, nodes, interp, strided, slabs, mixed, sems,
):
    copies = [
        pltpu.make_async_copy(interp_hbm, interp, sems.at[0]),
        pltpu.make_async_copy(data_hbm, data, sems.at[1]),
    ] + [
        pltpu.make_async_copy(node_hbm.at[k, :, strip(j)], nodes.at[k, j], sems.at[2 + 2 * k + j])
        for k in range(FIRST)
        for j in range(2)
    ]
    for copy in copies:
        copy.start()
    copies[0].wait()
    fill_weight(weight, interp)
    copies[1].wait()
    for j in range(4):
        strided[j] = data[:, strip(j)].astype(jnp.float32)

    def load_strided(w, columns):
        j = columns.start // STRIP
        parts = [strided[j + i, pl.ds(w, BOXES, stride=SLAB), :] for i in range(2)]
        return jnp.concatenate(parts, axis=1)

    def store_strided(w, columns, piece):
        j = columns.start // STRIP
        for i in range(2):
            strided[j + i, pl.ds(w, BOXES, stride=SLAB), :] = piece[:, strip(i)]

    def load(w, columns):
        return slabs[w * BOXES : (w + 1) * BOXES, columns]

    def store(w, columns, piece):
        slabs[w * BOXES : (w + 1) * BOXES, columns] = piece

    for k in range(FIRST):
        copies[2 + 2 * k].wait()
        copies[3 + 2 * k].wait()
        row_level(
            k,
            load if k else load_strided,
            store_strided if k == FIRST - 1 else store,
            nodes,
            cos_sin(box_ref[k]),
            mixed,
            weight,
        )
    for h in range(2):
        pair = [strided[2 * h + i].reshape(BOXES, SLAB, STRIP) for i in range(2)]
        out_ref[:, 2 * SLAB * h : 2 * SLAB * (h + 1), :] = jnp.concatenate(pair, axis=1).astype(
            jnp.bfloat16
        )
    phases = [
        box_ref[min(FIRST + k, LAST - 1)][:, strip(j)] for j in range(2) for k in range(SLAB)
    ]
    code = jnp.exp2(jnp.concatenate(phases, axis=0) * CODE).astype(jnp.bfloat16)
    out_ref[:, DATA:, :] = jnp.broadcast_to(code[None], (BOXES, 2 * SLAB, STRIP))


def first_levels(data, box_phase, node_phase, interp):
    return pl.pallas_call(
        first_kernel,
        in_specs=[HBM, VMEM, HBM, HBM],
        out_specs=[VMEM, VMEM],
        out_shape=[
            jax.ShapeDtypeStruct((BOXES, MESSAGE, STRIP), jnp.bfloat16),
            jax.ShapeDtypeStruct((2 * WIDTH, 2 * WIDTH), jnp.bfloat16),
        ],
        scratch_shapes=[
            pltpu.VMEM((ROWS, WIDTH), jnp.bfloat16),
            pltpu.VMEM((FIRST, 2, ROWS, STRIP), jnp.float32),
            pltpu.VMEM((2, 2, 2, NODES, NODES), jnp.bfloat16),
            pltpu.VMEM((4, ROWS, STRIP), jnp.float32),
            pltpu.VMEM((ROWS, WIDTH), jnp.float32),
            pltpu.VMEM((ROWS // 2, 2 * WIDTH), jnp.bfloat16),
            DMA((2 + 2 * FIRST,)),
        ],
        compiler_params=pltpu.CompilerParams(vmem_limit_bytes=58 << 20),
        cost_estimate=pl.CostEstimate(flops=3 << 30, bytes_accessed=8 << 20, transcendentals=0),
        name="levels0to2",
    )(data, box_phase, node_phase, interp)


def prep_kernel(
    box_ref, node_hbm, x_hbm, y_hbm, x_weight, y_weight, cos_ref, sin_ref, own_cos, own_sin,
    own, nodes, interps, sems,
):
    me = lax.axis_index("sx") * lax.axis_size("sy") + lax.axis_index("sy")
    rows = pl.ds(pl.multiple_of(me * SLAB, SLAB), SLAB)
    copies = [
        pltpu.make_async_copy(node_hbm.at[pl.ds(FIRST, INNER), rows, :], own, sems.at[0]),
        pltpu.make_async_copy(x_hbm, interps.at[0], sems.at[1]),
        pltpu.make_async_copy(y_hbm, interps.at[1], sems.at[2]),
    ] + [pltpu.make_async_copy(node_hbm.at[LAST + k], nodes.at[k], sems.at[3 + k]) for k in range(3)]
    for copy in copies:
        copy.start()
    copies[0].wait()
    own_cos[...], own_sin[...] = cos_sin(own[...])
    copies[1].wait()
    fill_weight(x_weight, interps.at[0])
    copies[2].wait()
    fill_weight(y_weight, interps.at[1])
    for k in range(3):
        copies[3 + k].wait()
        box_cos, box_sin = cos_sin(box_ref[LAST + k])
        for half in range(2):
            for start in range(0, ROWS // 2, CHUNK):
                ranges = pair_ranges(k, half, start, CHUNK)
                node_cos, node_sin = cos_sin(load_ranges(nodes.at[k], ranges, slice(None)))
                at = half * (ROWS // 2) + start
                cosine = node_cos * box_cos - node_sin * box_sin
                sine = node_sin * box_cos + node_cos * box_sin
                cos_ref[k, at : at + CHUNK, :] = cosine.astype(jnp.bfloat16)
                sin_ref[k, at : at + CHUNK, :] = sine.astype(jnp.bfloat16)


def prep(box_phase, node_phase, across_x, across_y):
    weight = jax.ShapeDtypeStruct((2 * WIDTH, 2 * WIDTH), jnp.bfloat16)
    table = jax.ShapeDtypeStruct((3, ROWS, NODES), jnp.bfloat16)
    own = jax.ShapeDtypeStruct((INNER, SLAB, NODES), jnp.float32)
    return pl.pallas_call(
        prep_kernel,
        in_specs=[VMEM, HBM, HBM, HBM],
        out_specs=[VMEM] * 6,
        out_shape=[weight, weight, table, table, own, own],
        scratch_shapes=[
            pltpu.VMEM((INNER, SLAB, NODES), jnp.float32),
            pltpu.VMEM((3, ROWS, NODES), jnp.float32),
            pltpu.VMEM((2, 2, 2, 2, NODES, NODES), jnp.bfloat16),
            DMA((6,)),
        ],
        compiler_params=pltpu.CompilerParams(vmem_limit_bytes=42 << 20),
        cost_estimate=pl.CostEstimate(flops=60_000_000, bytes_accessed=15 << 20, transcendentals=0),
        name="prep",
    )(box_phase, node_phase, across_x, across_y)


def multiply(bit, first, target, mixed, weight):
    for part in range(4):
        product = jnp.dot(
            mixed[first : first + BLOCK],
            weight[:, part * NODES : (part + 1) * NODES],
            preferred_element_type=jnp.float32,
        )
        at = 0
        for r, n in pair_ranges(bit, part >> 1, first, BLOCK):
            target[r : r + n, (RE, IM)[part & 1]] = product[at : at + n].astype(target.dtype)
            at += n


def inner_kernel(
    data_ref, own_cos, own_sin, x_weight, y_weight, out_ref, current, mixed, box_cos, box_sin
):
    for h in range(2):
        pair = data_ref[:, 2 * SLAB * h : 2 * SLAB * (h + 1), :].astype(jnp.float32)
        for i in range(2):
            piece = pair[:, i * SLAB : (i + 1) * SLAB, :]
            current[:, strip(2 * h + i)] = piece.reshape(ROWS, STRIP)
    code = data_ref[:, DATA:, :].astype(jnp.float32)
    box_cos[...], box_sin[...] = cos_sin(jnp.log2(code) * (1.0 / CODE))

    for k, bit in enumerate(BOX_BITS):
        target = out_ref if k == INNER - 1 else current
        weight = y_weight if SECOND[k] else x_weight
        for first in range(0, ROWS // 2, BLOCK):
            for half in range(2):
                for start in range(first, first + BLOCK, CHUNK):
                    rows = [
                        r + i
                        for r, n in pair_ranges(bit, half, start, CHUNK)
                        for i in range(0, n, SLAB)
                    ]
                    for j in range(2):
                        node_cos, node_sin = own_cos[k, :, strip(j)], own_sin[k, :, strip(j)]
                        re_parts, im_parts = [], []
                        for r in rows:
                            at = slice(SLAB * j + k, SLAB * j + k + 1)
                            c, s = box_cos[r // SLAB, at, :], box_sin[r // SLAB, at, :]
                            cosine = c * node_cos - s * node_sin
                            sine = s * node_cos + c * node_sin
                            re = current[r : r + SLAB, strip(j)]
                            im = current[r : r + SLAB, strip(2 + j)]
                            re_parts.append(re * cosine - im * sine)
                            im_parts.append(re * sine + im * cosine)
                        to = slice(start, start + CHUNK)
                        mixed[to, strip(4 * half + j)] = jnp.concatenate(re_parts, axis=0).astype(
                            jnp.bfloat16
                        )
                        mixed[to, strip(4 * half + 2 + j)] = jnp.concatenate(
                            im_parts, axis=0
                        ).astype(jnp.bfloat16)
            multiply(bit, first, target, mixed, weight)


def inner_levels(*operands):
    return pl.pallas_call(
        inner_kernel,
        in_specs=[VMEM] * len(operands),
        out_specs=VMEM,
        out_shape=jax.ShapeDtypeStruct((ROWS, WIDTH), jnp.bfloat16),
        scratch_shapes=[
            pltpu.VMEM((ROWS, WIDTH), jnp.float32),
            pltpu.VMEM((ROWS // 2, 2 * WIDTH), jnp.bfloat16),
            pltpu.VMEM((BOXES, 2 * SLAB, STRIP), jnp.float32),
            pltpu.VMEM((BOXES, 2 * SLAB, STRIP), jnp.float32),
        ],
        compiler_params=pltpu.CompilerParams(vmem_limit_bytes=32 << 20),
        cost_estimate=pl.CostEstimate(flops=7 << 30, bytes_accessed=8 << 20, transcendentals=0),
        name="levels3to9",
    )(*operands)


def outer_kernel(data_ref, cos_ref, sin_ref, weight, out_ref, current, mixed):
    current[...] = data_ref[...].astype(jnp.float32)
    for k in range(3):
        target = out_ref if k == 2 else current
        for first in range(0, ROWS // 2, BLOCK):
            for half in range(2):
                for start in range(first, first + BLOCK, CHUNK):
                    ranges = pair_ranges(k, half, start, CHUNK)
                    at = half * (ROWS // 2) + start
                    rotate_into(
                        mixed,
                        slice(start, start + CHUNK),
                        half,
                        load_ranges(current, ranges, RE),
                        load_ranges(current, ranges, IM),
                        cos_ref[k, at : at + CHUNK, :].astype(jnp.float32),
                        sin_ref[k, at : at + CHUNK, :].astype(jnp.float32),
                    )
            multiply(k, first, target, mixed, weight)


def outer_levels(*operands):
    return pl.pallas_call(
        outer_kernel,
        in_specs=[VMEM] * len(operands),
        out_specs=VMEM,
        out_shape=jax.ShapeDtypeStruct((ROWS, WIDTH), jnp.bfloat16),
        scratch_shapes=[
            pltpu.VMEM((ROWS, WIDTH), jnp.float32),
            pltpu.VMEM((ROWS // 2, 2 * WIDTH), jnp.bfloat16),
        ],
        compiler_params=pltpu.CompilerParams(vmem_limit_bytes=32 << 20),
        cost_estimate=pl.CostEstimate(flops=3 << 30, bytes_accessed=8 << 20, transcendentals=0),
        name="levels10to12",
    )(*operands)


def exchange(blocks):
    return lax.all_to_all(blocks, AXES, 0, 0, tiled=True)


def on_device(signal, box_phase, node_phase, local_interp, across_x, across_y):
    own = box_phase[:, 0]
    messages, local = first_levels(signal[0, 0], own, node_phase, local_interp)
    moved = exchange(messages)
    x_weight, y_weight, last_cos, last_sin, own_cos, own_sin = prep(
        own, node_phase, across_x, across_y
    )
    inner = inner_levels(moved, own_cos, own_sin, x_weight, y_weight)
    return outer_levels(exchange(inner), last_cos, last_sin, local)[None, None]


def solution(mesh):
    return jax.shard_map(
        on_device,
        mesh=mesh,
        in_specs=(P("sx", "sy", None, None), P(None, "sx", "sy", None), P(), P(), P(), P()),
        out_specs=P("sx", "sy", None, None),
        check_vma=False,
    )
```

```python
import functools

import jax
import jax.numpy as jnp
from jax import lax
from jax.experimental import pallas as pl
from jax.experimental.pallas import tpu as pltpu
from jax.sharding import PartitionSpec as P

AXES = ("sx", "sy")
ROWS = 1024
NODES = 256
WIDTH = 512
BOXES = 128
SLAB = 8
CHUNK = 64
HALF = ROWS // 2
STRIP = 128
CODE = 38.0
MESSAGE = 48
DATA = 32
FIRST = 3
INNER = 7
LAST = FIRST + INNER
BLOCK = 256
BOX_BITS = (4, 0, 5, 1, 6, 2, 3)
SECOND = (0, 1, 0, 1, 0, 1, 1)
SPLITS = (6, 6, 6, 5, 5, 5, 5)
SPLIT = 6

SIN = (9.99999996e-01, -1.66666580e-01, 8.33305063e-03, -1.98090465e-04, 2.60516562e-06)
COS = (9.99999953e-01, -4.99999051e-01, 4.16635791e-02, -1.38536671e-03, 2.31531671e-05)


def horner(coefficients, x):
    total = coefficients[-1] * x + coefficients[-2]
    for factor in coefficients[-3::-1]:
        total = total * x + factor
    return total


def cos_sin(angle):
    half = angle * 0.5
    square = half * half
    sine = half * horner(SIN, square)
    cosine = horner(COS, square)
    double = sine + sine
    return 1.0 - double * sine, double * cosine


def pair_slabs(bit, half, split, block):
    return [
        slab
        for slab in range(BOXES)
        if slab >> bit & 1 == half and slab >> split & 1 == block
    ]


def runs(slabs):
    found = []
    for i, slab in enumerate(slabs):
        if found and found[-1][1] + found[-1][2] == slab * SLAB:
            found[-1][2] += SLAB
        else:
            found.append([i * SLAB, slab * SLAB, SLAB])
    return found


def load_slabs(ref, slabs, columns):
    parts = [ref[r : r + n, columns] for _, r, n in runs(slabs)]
    return parts[0] if len(parts) == 1 else jnp.concatenate(parts, axis=0)


def interleave(major, minor):
    done = 0
    for i, step in enumerate(major):
        step()
        upto = len(minor) * (i + 1) // len(major)
        for other in minor[done:upto]:
            other()
        done = upto
    for other in minor[done:]:
        other()


def pipeline(levels, rotate, multiply, apart=()):
    stages = [(k, block) for k in range(levels) for block in range(2)]
    ready = rotate(*stages[0])
    for i, stage in enumerate(stages):
        if i == 0 or stage in apart:
            interleave(ready, [])
        after = stages[i + 1] if i + 1 < len(stages) else None
        ready = rotate(*after) if after else []
        interleave(multiply(*stage), [] if after in apart else ready)


RE = slice(0, NODES)
IM = slice(NODES, WIDTH)


VMEM = pl.BlockSpec(memory_space=pltpu.VMEM)
HBM = pl.BlockSpec(memory_space=pltpu.HBM)
DMA = pltpu.SemaphoreType.DMA


def negate(negated, interp):
    for child in range(2):
        for source in range(2):
            negated[child, source] = -interp[child, source, 1]


def product(mixed, block, child, imaginary, interp, negated):
    rows = slice(block * BLOCK, (block + 1) * BLOCK)
    total = None
    for source in range(2):
        left = source * WIDTH
        if imaginary:
            first, second = interp[child, source, 1], interp[child, source, 0]
        else:
            first, second = interp[child, source, 0], negated[child, source]
        for columns, matrix in (
            (slice(left, left + NODES), first),
            (slice(left + NODES, left + WIDTH), second),
        ):
            term = jnp.dot(mixed[rows, columns], matrix, preferred_element_type=jnp.float32)
            total = term if total is None else total + term
    return total


def strip(j):
    return slice(j * STRIP, (j + 1) * STRIP)


def rotate_into(mixed, rows, half, re, im, c, s):
    left = half * WIDTH
    mixed[rows, left : left + NODES] = (re * c - im * s).astype(jnp.bfloat16)
    mixed[rows, left + NODES : left + WIDTH] = (re * s + im * c).astype(jnp.bfloat16)


def first_kernel(
    data_hbm, box_ref, node_hbm, interp_hbm, out_hbm,
    data, nodes, interp, negated, current, mixed, messages, sems,
):
    copies = [
        pltpu.make_async_copy(node_hbm.at[0], nodes.at[0], sems.at[0]),
        pltpu.make_async_copy(data_hbm, data, sems.at[1]),
        pltpu.make_async_copy(interp_hbm, interp, sems.at[2]),
    ] + [pltpu.make_async_copy(node_hbm.at[k], nodes.at[k], sems.at[2 + k]) for k in (1, 2)]
    for copy in copies:
        copy.start()
    boxes = [cos_sin(box_ref[k]) for k in range(FIRST)]
    phases = [
        box_ref[min(FIRST + k, LAST - 1)][:, strip(j)] for j in range(2) for k in range(SLAB)
    ]
    code = jnp.exp2(jnp.concatenate(phases, axis=0) * CODE).astype(jnp.bfloat16)
    messages[:, DATA:, :] = jnp.broadcast_to(code[None], (BOXES, 2 * SLAB, STRIP))
    copies[0].wait()
    copies[1].wait()

    def swap(bit, zero, one):
        distance = 1 << bit
        at_zero = lax.broadcasted_iota(jnp.int32, zero.shape, 1) & distance == 0
        return (
            jnp.where(at_zero, zero, pltpu.roll(one, distance, 1)),
            jnp.where(at_zero, pltpu.roll(zero, SLAB - distance, 1), one),
        )

    def rotate_rows(k, block, i, j):
        sides = []
        for side in range(2):
            first = block * HALF + side * BLOCK + i * CHUNK
            rows = slice(first, first + CHUNK)
            node_cos, node_sin = cos_sin(nodes[k, rows, strip(j)])
            box_cos, box_sin = boxes[k][0][:, strip(j)], boxes[k][1][:, strip(j)]
            c = node_cos * box_cos - node_sin * box_sin
            s = node_sin * box_cos + node_cos * box_sin
            source = current if k else data
            re = source[rows, strip(j)].astype(jnp.float32)
            im = source[rows, strip(2 + j)].astype(jnp.float32)
            sides.append((re * c - im * s, re * s + im * c))
        at = block * BLOCK + i * CHUNK
        for part in range(2):
            pair = [side[part].reshape(CHUNK // SLAB, SLAB, STRIP) for side in sides]
            for half, rows in enumerate(swap(k, *pair)):
                mixed[at : at + CHUNK, strip(4 * half + 2 * part + j)] = rows.reshape(
                    CHUNK, STRIP
                ).astype(jnp.bfloat16)

    def rotate(k, block):
        if k and block == 0:
            copies[2 + k].wait()
        return [
            functools.partial(rotate_rows, k, block, i, j)
            for i in range(BLOCK // CHUNK)
            for j in range(2)
        ]

    def multiply_part(k, block, part):
        pair = [
            product(mixed, block, child, part, interp, negated).reshape(
                BLOCK // SLAB, SLAB, NODES
            )
            for child in range(2)
        ]
        for side, rows in enumerate(swap(k, *pair)):
            if k < FIRST - 1:
                first = block * HALF + side * BLOCK
                current[first : first + BLOCK, (RE, IM)[part]] = rows.reshape(BLOCK, NODES)
            else:
                first = (block * HALF + side * BLOCK) // SLAB
                both = jnp.concatenate([rows[:, :, strip(0)], rows[:, :, strip(1)]], axis=1)
                messages[
                    first : first + BLOCK // SLAB, 2 * SLAB * part : 2 * SLAB * (part + 1), :
                ] = both.astype(jnp.bfloat16)

    def multiply(k, block):
        if k == 0 and block == 0:
            copies[2].wait()
            negate(negated, interp)
        return [functools.partial(multiply_part, k, block, part) for part in range(2)] + [
            functools.partial(leave, k, block)
        ]

    leaving = [
        pltpu.make_async_copy(
            messages.at[pl.ds(block * CHUNK, CHUNK)],
            out_hbm.at[pl.ds(block * CHUNK, CHUNK)],
            sems.at[5 + block],
        )
        for block in range(2)
    ]

    def leave(k, block):
        if k == FIRST - 1:
            leaving[block].start()

    pipeline(FIRST, rotate, multiply)
    for copy in leaving:
        copy.wait()


def first_levels(data, box_phase, node_phase, interp):
    return pl.pallas_call(
        first_kernel,
        in_specs=[HBM, VMEM, HBM, HBM],
        out_specs=HBM,
        out_shape=jax.ShapeDtypeStruct((BOXES, MESSAGE, STRIP), jnp.bfloat16),
        scratch_shapes=[
            pltpu.VMEM((ROWS, WIDTH), jnp.bfloat16),
            pltpu.VMEM((FIRST, ROWS, NODES), jnp.float32),
            pltpu.VMEM((2, 2, 2, NODES, NODES), jnp.bfloat16),
            pltpu.VMEM((2, 2, NODES, NODES), jnp.bfloat16),
            pltpu.VMEM((ROWS, WIDTH), jnp.float32),
            pltpu.VMEM((ROWS // 2, 2 * WIDTH), jnp.bfloat16),
            pltpu.VMEM((BOXES, MESSAGE, STRIP), jnp.bfloat16),
            DMA((7,)),
        ],
        compiler_params=pltpu.CompilerParams(vmem_limit_bytes=58 << 20),
        cost_estimate=pl.CostEstimate(flops=3 << 30, bytes_accessed=8 << 20, transcendentals=0),
        name="levels0to2",
    )(data, box_phase, node_phase, interp)


def prep_kernel(box_ref, node_hbm, cos_ref, sin_ref, own_cos, own_sin, own, nodes, sems):
    me = lax.axis_index("sx") * lax.axis_size("sy") + lax.axis_index("sy")
    rows = pl.ds(pl.multiple_of(me * SLAB, SLAB), SLAB)
    copies = [
        pltpu.make_async_copy(node_hbm.at[pl.ds(FIRST, INNER), rows, :], own, sems.at[0]),
    ] + [pltpu.make_async_copy(node_hbm.at[LAST + k], nodes.at[k], sems.at[1 + k]) for k in range(3)]
    for copy in copies:
        copy.start()
    copies[0].wait()
    own_cos[...], own_sin[...] = cos_sin(own[...])
    for k in range(3):
        copies[1 + k].wait()
        box_cos, box_sin = cos_sin(box_ref[LAST + k])
        for half in range(2):
            for block in range(2):
                slabs = pair_slabs(k, half, SPLIT, block)
                for i in range(0, len(slabs), SLAB):
                    angles = load_slabs(nodes.at[k], slabs[i : i + SLAB], slice(None))
                    node_cos, node_sin = cos_sin(angles)
                    at = half * HALF + block * BLOCK + i * SLAB
                    cosine = node_cos * box_cos - node_sin * box_sin
                    sine = node_sin * box_cos + node_cos * box_sin
                    cos_ref[k, at : at + CHUNK, :] = cosine.astype(jnp.bfloat16)
                    sin_ref[k, at : at + CHUNK, :] = sine.astype(jnp.bfloat16)


def prep(box_phase, node_phase):
    table = jax.ShapeDtypeStruct((3, ROWS, NODES), jnp.bfloat16)
    own = jax.ShapeDtypeStruct((INNER, SLAB, NODES), jnp.float32)
    return pl.pallas_call(
        prep_kernel,
        in_specs=[VMEM, HBM],
        out_specs=[VMEM] * 4,
        out_shape=[table, table, own, own],
        scratch_shapes=[
            pltpu.VMEM((INNER, SLAB, NODES), jnp.float32),
            pltpu.VMEM((3, ROWS, NODES), jnp.float32),
            DMA((4,)),
        ],
        compiler_params=pltpu.CompilerParams(vmem_limit_bytes=52 << 20),
        cost_estimate=pl.CostEstimate(flops=60_000_000, bytes_accessed=7 << 20, transcendentals=0),
        name="prep",
    )(box_phase, node_phase)


def multiply_part(bit, split, block, part, target, mixed, interp, negated):
    child, imaginary = part >> 1, part & 1
    total = product(mixed, block, child, imaginary, interp, negated)
    for at, r, n in runs(pair_slabs(bit, child, split, block)):
        target[r : r + n, (RE, IM)[imaginary]] = total[at : at + n].astype(target.dtype)


def inner_kernel(
    data_ref, own_cos, own_sin, x_hbm, y_hbm, out_ref,
    current, mixed, box_cos, box_sin, interps, negated, sems,
):
    copies = [
        pltpu.make_async_copy(hbm, interps.at[i], sems.at[i]) for i, hbm in enumerate((x_hbm, y_hbm))
    ]
    for copy in copies:
        copy.start()

    def receive(block, part):
        boxes = slice(block * CHUNK, (block + 1) * CHUNK)
        if part == 2:
            phase = jnp.log2(data_ref[boxes, DATA:, :].astype(jnp.float32)) * (1.0 / CODE)
            box_cos[boxes], box_sin[boxes] = cos_sin(phase)
        else:
            pair = data_ref[boxes, 2 * SLAB * part : 2 * SLAB * (part + 1), :].astype(jnp.float32)
            for i in range(2):
                piece = pair[:, i * SLAB : (i + 1) * SLAB, :]
                current[block * HALF : (block + 1) * HALF, strip(2 * part + i)] = piece.reshape(
                    HALF, STRIP
                )

    def rotate_slabs(k, block, half, i, j):
        slabs = pair_slabs(BOX_BITS[k], half, SPLITS[k], block)[i : i + SLAB]
        node_cos, node_sin = own_cos[k, :, strip(j)], own_sin[k, :, strip(j)]
        at = slice(SLAB * j + k, SLAB * j + k + 1)
        re_parts, im_parts = [], []
        for slab in slabs:
            c, s = box_cos[slab, at, :], box_sin[slab, at, :]
            cosine = c * node_cos - s * node_sin
            sine = s * node_cos + c * node_sin
            rows = slice(slab * SLAB, (slab + 1) * SLAB)
            re, im = current[rows, strip(j)], current[rows, strip(2 + j)]
            re_parts.append(re * cosine - im * sine)
            im_parts.append(re * sine + im * cosine)
        first = block * BLOCK + i * SLAB
        to = slice(first, first + CHUNK)
        for parts, column in ((re_parts, j), (im_parts, 2 + j)):
            joined = jnp.concatenate(parts, axis=0).astype(jnp.bfloat16)
            mixed[to, strip(4 * half + column)] = joined

    def rotate(k, block):
        if k == 1 and block == 0:
            copies[1].wait()
            negate(negated.at[1], interps.at[1])
        arrive = [functools.partial(receive, block, part) for part in range(3)] if k == 0 else []
        return arrive + [
            functools.partial(rotate_slabs, k, block, half, i, j)
            for half in range(2)
            for i in range(0, BLOCK // SLAB, SLAB)
            for j in range(2)
        ]

    def multiply(k, block):
        target = out_ref if k == INNER - 1 else current
        if k == 0 and block == 0:
            copies[0].wait()
            negate(negated.at[0], interps.at[0])
        return [
            functools.partial(
                multiply_part, BOX_BITS[k], SPLITS[k], block, part, target, mixed,
                interps.at[SECOND[k]], negated.at[SECOND[k]],
            )
            for part in range(4)
        ]

    pipeline(INNER, rotate, multiply, apart=[(3, 0)])


def inner_levels(*operands):
    return pl.pallas_call(
        inner_kernel,
        in_specs=[VMEM] * 3 + [HBM] * 2,
        out_specs=VMEM,
        out_shape=jax.ShapeDtypeStruct((ROWS, WIDTH), jnp.bfloat16),
        scratch_shapes=[
            pltpu.VMEM((ROWS, WIDTH), jnp.float32),
            pltpu.VMEM((ROWS // 2, 2 * WIDTH), jnp.bfloat16),
            pltpu.VMEM((BOXES, 2 * SLAB, STRIP), jnp.float32),
            pltpu.VMEM((BOXES, 2 * SLAB, STRIP), jnp.float32),
            pltpu.VMEM((2, 2, 2, 2, NODES, NODES), jnp.bfloat16),
            pltpu.VMEM((2, 2, 2, NODES, NODES), jnp.bfloat16),
            DMA((2,)),
        ],
        compiler_params=pltpu.CompilerParams(vmem_limit_bytes=52 << 20),
        cost_estimate=pl.CostEstimate(flops=7 << 30, bytes_accessed=8 << 20, transcendentals=0),
        name="levels3to9",
    )(*operands)


def outer_kernel(
    data_ref, cos_ref, sin_ref, interp, out_hbm, current, mixed, negated, result, sems
):
    negate(negated, interp)

    def receive(block):
        rows = slice(block * HALF, (block + 1) * HALF)
        current[rows] = data_ref[rows].astype(jnp.float32)

    leaving = [
        pltpu.make_async_copy(
            result.at[pl.ds(block * HALF, HALF)],
            out_hbm.at[pl.ds(block * HALF, HALF)],
            sems.at[block],
        )
        for block in range(2)
    ]

    def rotate_slabs(k, block, half, i):
        slabs = pair_slabs(k, half, SPLIT, block)[i : i + SLAB]
        first = block * BLOCK + i * SLAB
        at = half * HALF + first
        rotate_into(
            mixed,
            slice(first, first + CHUNK),
            half,
            load_slabs(current, slabs, RE),
            load_slabs(current, slabs, IM),
            cos_ref[k, at : at + CHUNK, :].astype(jnp.float32),
            sin_ref[k, at : at + CHUNK, :].astype(jnp.float32),
        )

    def rotate(k, block):
        arrive = [functools.partial(receive, block)] if k == 0 else []
        return arrive + [
            functools.partial(rotate_slabs, k, block, half, i)
            for half in range(2)
            for i in range(0, BLOCK // SLAB, SLAB)
        ]

    def multiply(k, block):
        target = result if k == 2 else current
        parts = [
            functools.partial(
                multiply_part, k, SPLIT, block, part, target, mixed, interp, negated
            )
            for part in range(4)
        ]
        return parts + [leaving[block].start] if k == 2 else parts

    pipeline(3, rotate, multiply)
    for copy in leaving:
        copy.wait()


def outer_levels(*operands):
    return pl.pallas_call(
        outer_kernel,
        in_specs=[VMEM] * len(operands),
        out_specs=HBM,
        out_shape=jax.ShapeDtypeStruct((ROWS, WIDTH), jnp.bfloat16),
        scratch_shapes=[
            pltpu.VMEM((ROWS, WIDTH), jnp.float32),
            pltpu.VMEM((ROWS // 2, 2 * WIDTH), jnp.bfloat16),
            pltpu.VMEM((2, 2, NODES, NODES), jnp.bfloat16),
            pltpu.VMEM((ROWS, WIDTH), jnp.bfloat16),
            DMA((2,)),
        ],
        compiler_params=pltpu.CompilerParams(vmem_limit_bytes=32 << 20),
        cost_estimate=pl.CostEstimate(flops=3 << 30, bytes_accessed=8 << 20, transcendentals=0),
        name="levels10to12",
    )(*operands)


def exchange(blocks):
    return lax.all_to_all(blocks, AXES, 0, 0, tiled=True)


def on_device(signal, box_phase, node_phase, local_interp, across_x, across_y):
    own = box_phase[:, 0]
    moved = exchange(first_levels(signal[0, 0], own, node_phase, local_interp))
    last_cos, last_sin, own_cos, own_sin = prep(own, node_phase)
    inner = inner_levels(moved, own_cos, own_sin, across_x, across_y)
    return outer_levels(exchange(inner), last_cos, last_sin, local_interp)[None, None]


def solution(mesh):
    return jax.shard_map(
        on_device,
        mesh=mesh,
        in_specs=(P("sx", "sy", None, None), P(None, "sx", "sy", None), P(), P(), P(), P()),
        out_specs=P("sx", "sy", None, None),
        check_vma=False,
    )
```

```python
import functools

import jax
import jax.numpy as jnp
from jax import lax
from jax.experimental import pallas as pl
from jax.experimental.pallas import tpu as pltpu
from jax.sharding import PartitionSpec as P

AXES = ("sx", "sy")
ROWS = 1024
NODES = 256
WIDTH = 512
BOXES = 128
SLAB = 8
CHUNK = 64
HALF = ROWS // 2
STRIP = 128
CODE = 38.0
MESSAGE = 48
DATA = 32
FIRST = 3
INNER = 7
LAST = FIRST + INNER
BLOCK = 256
BOX_BITS = (4, 0, 5, 1, 6, 2, 3)
SECOND = (0, 1, 0, 1, 0, 1, 1)
SPLITS = (6, 6, 6, 5, 5, 5, 5)
SPLIT = 6

SIN = (9.99999242e-01, -1.66656797e-01, 8.31322541e-03, -1.85234428e-04)
COS = (0.99999325, -0.49991211, 0.04148738, -0.00127111)


def horner(coefficients, x):
    total = coefficients[-1] * x + coefficients[-2]
    for factor in coefficients[-3::-1]:
        total = total * x + factor
    return total


def cos_sin(angle):
    half = angle * 0.5
    square = half * half
    sine = half * horner(SIN, square)
    cosine = horner(COS, square)
    double = sine + sine
    return 1.0 - double * sine, double * cosine


def pair_slabs(bit, half, split, block):
    return [
        slab
        for slab in range(BOXES)
        if slab >> bit & 1 == half and slab >> split & 1 == block
    ]


def runs(slabs):
    found = []
    for i, slab in enumerate(slabs):
        if found and found[-1][1] + found[-1][2] == slab * SLAB:
            found[-1][2] += SLAB
        else:
            found.append([i * SLAB, slab * SLAB, SLAB])
    return found


def load_slabs(ref, slabs, columns):
    parts = [ref[r : r + n, columns] for _, r, n in runs(slabs)]
    return parts[0] if len(parts) == 1 else jnp.concatenate(parts, axis=0)


def interleave(major, minor):
    done = 0
    for i, step in enumerate(major):
        step()
        upto = len(minor) * (i + 1) // len(major)
        for other in minor[done:upto]:
            other()
        done = upto
    for other in minor[done:]:
        other()


def pipeline(levels, rotate, multiply, apart=()):
    stages = [(k, block) for k in range(levels) for block in range(2)]
    ready = rotate(*stages[0])
    for i, stage in enumerate(stages):
        if i == 0 or stage in apart:
            interleave(ready, [])
        after = stages[i + 1] if i + 1 < len(stages) else None
        ready = rotate(*after) if after else []
        interleave(multiply(*stage), [] if after in apart else ready)


RE = slice(0, NODES)
IM = slice(NODES, WIDTH)


VMEM = pl.BlockSpec(memory_space=pltpu.VMEM)
HBM = pl.BlockSpec(memory_space=pltpu.HBM)
DMA = pltpu.SemaphoreType.DMA


def fill_weight(weight, interp):
    for child in range(2):
        for source in range(2):
            r, c = source * WIDTH, child * WIDTH
            real, imag = interp[child, source, 0], interp[child, source, 1]
            weight[r : r + NODES, c : c + NODES] = real
            weight[r : r + NODES, c + NODES : c + WIDTH] = imag
            weight[r + NODES : r + WIDTH, c : c + NODES] = -imag
            weight[r + NODES : r + WIDTH, c + NODES : c + WIDTH] = real


def product(mixed, block, part, weight):
    return jnp.dot(
        mixed[block * BLOCK : (block + 1) * BLOCK],
        weight[:, part * NODES : (part + 1) * NODES],
        preferred_element_type=jnp.float32,
    )


def strip(j):
    return slice(j * STRIP, (j + 1) * STRIP)


def rotate_into(mixed, rows, half, re, im, c, s):
    left = half * WIDTH
    mixed[rows, left : left + NODES] = (re * c - im * s).astype(jnp.bfloat16)
    mixed[rows, left + NODES : left + WIDTH] = (re * s + im * c).astype(jnp.bfloat16)


def first_kernel(
    data_hbm, box_ref, node_hbm, interp_hbm, out_hbm,
    data, nodes, interp, weight, cosines, sines, current, mixed, messages, sems,
):
    copies = [
        pltpu.make_async_copy(node_hbm.at[0], nodes.at[0], sems.at[0]),
        pltpu.make_async_copy(interp_hbm, interp, sems.at[1]),
        pltpu.make_async_copy(data_hbm, data, sems.at[2]),
    ] + [pltpu.make_async_copy(node_hbm.at[k], nodes.at[k], sems.at[2 + k]) for k in (1, 2)]
    for copy in copies:
        copy.start()
    boxes = [cos_sin(box_ref[k]) for k in range(FIRST)]
    phases = [
        box_ref[min(FIRST + k, LAST - 1)][:, strip(j)] for j in range(2) for k in range(SLAB)
    ]
    code = jnp.exp2(jnp.concatenate(phases, axis=0) * CODE).astype(jnp.bfloat16)
    messages[:, DATA:, :] = jnp.broadcast_to(code[None], (BOXES, 2 * SLAB, STRIP))

    def turn(k, rows, columns):
        node_cos, node_sin = cos_sin(nodes[k, rows, columns])
        box_cos, box_sin = boxes[k][0][:, columns], boxes[k][1][:, columns]
        return node_cos * box_cos - node_sin * box_sin, node_sin * box_cos + node_cos * box_sin

    copies[0].wait()
    for first in range(0, ROWS, CHUNK):
        for j in range(2):
            rows = slice(first, first + CHUNK)
            cosines[rows, strip(j)], sines[rows, strip(j)] = turn(0, rows, strip(j))
    copies[1].wait()
    fill_weight(weight, interp)
    copies[2].wait()

    def swap(bit, zero, one):
        distance = 1 << bit
        at_zero = lax.broadcasted_iota(jnp.int32, zero.shape, 1) & distance == 0
        return (
            jnp.where(at_zero, zero, pltpu.roll(one, distance, 1)),
            jnp.where(at_zero, pltpu.roll(zero, SLAB - distance, 1), one),
        )

    def rotate_rows(k, block, i, j):
        sides = []
        for side in range(2):
            first = block * HALF + side * BLOCK + i * CHUNK
            rows = slice(first, first + CHUNK)
            if k:
                c, s = turn(k, rows, strip(j))
            else:
                c, s = cosines[rows, strip(j)], sines[rows, strip(j)]
            source = current if k else data
            re = source[rows, strip(j)].astype(jnp.float32)
            im = source[rows, strip(2 + j)].astype(jnp.float32)
            sides.append((re * c - im * s, re * s + im * c))
        at = block * BLOCK + i * CHUNK
        for part in range(2):
            pair = [side[part].reshape(CHUNK // SLAB, SLAB, STRIP) for side in sides]
            for half, rows in enumerate(swap(k, *pair)):
                mixed[at : at + CHUNK, strip(4 * half + 2 * part + j)] = rows.reshape(
                    CHUNK, STRIP
                ).astype(jnp.bfloat16)

    def rotate(k, block):
        if k and block == 0:
            copies[2 + k].wait()
        return [
            functools.partial(rotate_rows, k, block, i, j)
            for i in range(BLOCK // CHUNK)
            for j in range(2)
        ]

    def multiply_part(k, block, part):
        pair = [
            product(mixed, block, 2 * child + part, weight).reshape(
                BLOCK // SLAB, SLAB, NODES
            )
            for child in range(2)
        ]
        for side, rows in enumerate(swap(k, *pair)):
            if k < FIRST - 1:
                first = block * HALF + side * BLOCK
                current[first : first + BLOCK, (RE, IM)[part]] = rows.reshape(BLOCK, NODES)
            else:
                first = (block * HALF + side * BLOCK) // SLAB
                both = jnp.concatenate([rows[:, :, strip(0)], rows[:, :, strip(1)]], axis=1)
                messages[
                    first : first + BLOCK // SLAB, 2 * SLAB * part : 2 * SLAB * (part + 1), :
                ] = both.astype(jnp.bfloat16)

    def multiply(k, block):
        return [functools.partial(multiply_part, k, block, part) for part in range(2)] + [
            functools.partial(leave, k, block)
        ]

    leaving = [
        pltpu.make_async_copy(
            messages.at[pl.ds(block * CHUNK, CHUNK)],
            out_hbm.at[pl.ds(block * CHUNK, CHUNK)],
            sems.at[5 + block],
        )
        for block in range(2)
    ]

    def leave(k, block):
        if k == FIRST - 1:
            leaving[block].start()

    pipeline(FIRST, rotate, multiply)
    for copy in leaving:
        copy.wait()


def first_levels(data, box_phase, node_phase, interp):
    return pl.pallas_call(
        first_kernel,
        in_specs=[HBM, VMEM, HBM, HBM],
        out_specs=HBM,
        out_shape=jax.ShapeDtypeStruct((BOXES, MESSAGE, STRIP), jnp.bfloat16),
        scratch_shapes=[
            pltpu.VMEM((ROWS, WIDTH), jnp.bfloat16),
            pltpu.VMEM((FIRST, ROWS, NODES), jnp.float32),
            pltpu.VMEM((2, 2, 2, NODES, NODES), jnp.bfloat16),
            pltpu.VMEM((2 * WIDTH, 2 * WIDTH), jnp.bfloat16),
            pltpu.VMEM((ROWS, NODES), jnp.float32),
            pltpu.VMEM((ROWS, NODES), jnp.float32),
            pltpu.VMEM((ROWS, WIDTH), jnp.float32),
            pltpu.VMEM((ROWS // 2, 2 * WIDTH), jnp.bfloat16),
            pltpu.VMEM((BOXES, MESSAGE, STRIP), jnp.bfloat16),
            DMA((7,)),
        ],
        compiler_params=pltpu.CompilerParams(vmem_limit_bytes=58 << 20),
        cost_estimate=pl.CostEstimate(flops=3 << 30, bytes_accessed=8 << 20, transcendentals=0),
        name="levels0to2",
    )(data, box_phase, node_phase, interp)


def prep_kernel(
    box_ref, node_hbm, local_hbm, x_hbm, y_hbm,
    cos_ref, sin_ref, own_cos, own_sin, local_weight, x_weight, y_weight,
    own, nodes, interps, sems,
):
    me = lax.axis_index("sx") * lax.axis_size("sy") + lax.axis_index("sy")
    rows = pl.ds(pl.multiple_of(me * SLAB, SLAB), SLAB)
    copies = [
        pltpu.make_async_copy(node_hbm.at[pl.ds(FIRST, INNER), rows, :], own, sems.at[0]),
    ] + [pltpu.make_async_copy(node_hbm.at[LAST + k], nodes.at[k], sems.at[1 + k]) for k in range(3)]
    copies += [
        pltpu.make_async_copy(hbm, interps.at[k], sems.at[4 + k])
        for k, hbm in enumerate((x_hbm, y_hbm, local_hbm))
    ]
    for copy in copies:
        copy.start()
    copies[0].wait()
    own_cos[...], own_sin[...] = cos_sin(own[...])
    for k, weight in enumerate((x_weight, y_weight, local_weight)):
        copies[4 + k].wait()
        fill_weight(weight, interps.at[k])
    for k in range(3):
        copies[1 + k].wait()
        box_cos, box_sin = cos_sin(box_ref[LAST + k])
        for half in range(2):
            for block in range(2):
                slabs = pair_slabs(k, half, SPLIT, block)
                for i in range(0, len(slabs), SLAB):
                    angles = load_slabs(nodes.at[k], slabs[i : i + SLAB], slice(None))
                    node_cos, node_sin = cos_sin(angles)
                    at = half * HALF + block * BLOCK + i * SLAB
                    cosine = node_cos * box_cos - node_sin * box_sin
                    sine = node_sin * box_cos + node_cos * box_sin
                    cos_ref[k, at : at + CHUNK, :] = cosine.astype(jnp.bfloat16)
                    sin_ref[k, at : at + CHUNK, :] = sine.astype(jnp.bfloat16)


def prep(box_phase, node_phase, *interps):
    weight = jax.ShapeDtypeStruct((2 * WIDTH, 2 * WIDTH), jnp.bfloat16)
    table = jax.ShapeDtypeStruct((3, ROWS, NODES), jnp.bfloat16)
    own = jax.ShapeDtypeStruct((INNER, SLAB, NODES), jnp.float32)
    return pl.pallas_call(
        prep_kernel,
        in_specs=[VMEM] + [HBM] * 4,
        out_specs=[VMEM] * 7,
        out_shape=[table, table, own, own, weight, weight, weight],
        scratch_shapes=[
            pltpu.VMEM((INNER, SLAB, NODES), jnp.float32),
            pltpu.VMEM((3, ROWS, NODES), jnp.float32),
            pltpu.VMEM((3, 2, 2, 2, NODES, NODES), jnp.bfloat16),
            DMA((7,)),
        ],
        compiler_params=pltpu.CompilerParams(vmem_limit_bytes=52 << 20),
        cost_estimate=pl.CostEstimate(flops=60_000_000, bytes_accessed=7 << 20, transcendentals=0),
        name="prep",
    )(box_phase, node_phase, *interps)


def multiply_part(bit, split, block, part, target, mixed, weight):
    total = product(mixed, block, part, weight)
    for at, r, n in runs(pair_slabs(bit, part >> 1, split, block)):
        target[r : r + n, (RE, IM)[part & 1]] = total[at : at + n].astype(target.dtype)


def inner_kernel(
    data_ref, own_cos, own_sin, x_hbm, y_hbm, out_ref,
    current, mixed, box_cos, box_sin, weights, sems,
):
    copies = [
        pltpu.make_async_copy(hbm, weights.at[i], sems.at[i]) for i, hbm in enumerate((x_hbm, y_hbm))
    ]
    copies[0].start()

    def receive(block, part):
        boxes = slice(block * CHUNK, (block + 1) * CHUNK)
        if part == 2:
            phase = jnp.log2(data_ref[boxes, DATA:, :].astype(jnp.float32)) * (1.0 / CODE)
            box_cos[boxes], box_sin[boxes] = cos_sin(phase)
        else:
            pair = data_ref[boxes, 2 * SLAB * part : 2 * SLAB * (part + 1), :].astype(jnp.float32)
            for i in range(2):
                piece = pair[:, i * SLAB : (i + 1) * SLAB, :]
                current[block * HALF : (block + 1) * HALF, strip(2 * part + i)] = piece.reshape(
                    HALF, STRIP
                )

    def rotate_slabs(k, block, half, i, j):
        slabs = pair_slabs(BOX_BITS[k], half, SPLITS[k], block)[i : i + SLAB]
        node_cos, node_sin = own_cos[k, :, strip(j)], own_sin[k, :, strip(j)]
        at = slice(SLAB * j + k, SLAB * j + k + 1)
        re_parts, im_parts = [], []
        for slab in slabs:
            c, s = box_cos[slab, at, :], box_sin[slab, at, :]
            cosine = c * node_cos - s * node_sin
            sine = s * node_cos + c * node_sin
            rows = slice(slab * SLAB, (slab + 1) * SLAB)
            re, im = current[rows, strip(j)], current[rows, strip(2 + j)]
            re_parts.append(re * cosine - im * sine)
            im_parts.append(re * sine + im * cosine)
        first = block * BLOCK + i * SLAB
        to = slice(first, first + CHUNK)
        for parts, column in ((re_parts, j), (im_parts, 2 + j)):
            joined = jnp.concatenate(parts, axis=0).astype(jnp.bfloat16)
            mixed[to, strip(4 * half + column)] = joined

    def rotate(k, block):
        steps = [
            functools.partial(rotate_slabs, k, block, half, i, j)
            for half in range(2)
            for i in range(0, BLOCK // SLAB, SLAB)
            for j in range(2)
        ]
        if k:
            return steps
        steps = [functools.partial(receive, block, part) for part in range(3)] + steps
        return steps + [copies[1].start] + rotate(0, 1) if block == 0 else steps

    def multiply(k, block):
        target = out_ref if k == INNER - 1 else current
        if k < 2 and block == 0:
            copies[k].wait()
        return [
            functools.partial(
                multiply_part, BOX_BITS[k], SPLITS[k], block, part, target, mixed,
                weights.at[SECOND[k]],
            )
            for part in range(4)
        ]

    def rotate_later(k, block):
        return [] if (k, block) == (0, 1) else rotate(k, block)

    pipeline(INNER, rotate_later, multiply, apart=[(3, 0)])


def inner_levels(*operands):
    return pl.pallas_call(
        inner_kernel,
        in_specs=[VMEM] * 3 + [HBM] * 2,
        out_specs=VMEM,
        out_shape=jax.ShapeDtypeStruct((ROWS, WIDTH), jnp.bfloat16),
        scratch_shapes=[
            pltpu.VMEM((ROWS, WIDTH), jnp.float32),
            pltpu.VMEM((ROWS // 2, 2 * WIDTH), jnp.bfloat16),
            pltpu.VMEM((BOXES, 2 * SLAB, STRIP), jnp.float32),
            pltpu.VMEM((BOXES, 2 * SLAB, STRIP), jnp.float32),
            pltpu.VMEM((2, 2 * WIDTH, 2 * WIDTH), jnp.bfloat16),
            DMA((2,)),
        ],
        compiler_params=pltpu.CompilerParams(vmem_limit_bytes=52 << 20),
        cost_estimate=pl.CostEstimate(flops=7 << 30, bytes_accessed=8 << 20, transcendentals=0),
        name="levels3to9",
    )(*operands)


def outer_kernel(
    data_ref, cos_ref, sin_ref, weight, out_hbm, current, mixed, result, sems
):
    def receive(block):
        rows = slice(block * HALF, (block + 1) * HALF)
        current[rows] = data_ref[rows].astype(jnp.float32)

    leaving = [
        pltpu.make_async_copy(
            result.at[pl.ds(block * HALF, HALF)],
            out_hbm.at[pl.ds(block * HALF, HALF)],
            sems.at[block],
        )
        for block in range(2)
    ]

    def rotate_slabs(k, block, half, i):
        slabs = pair_slabs(k, half, SPLIT, block)[i : i + SLAB]
        first = block * BLOCK + i * SLAB
        at = half * HALF + first
        rotate_into(
            mixed,
            slice(first, first + CHUNK),
            half,
            load_slabs(current, slabs, RE),
            load_slabs(current, slabs, IM),
            cos_ref[k, at : at + CHUNK, :].astype(jnp.float32),
            sin_ref[k, at : at + CHUNK, :].astype(jnp.float32),
        )

    def rotate(k, block):
        arrive = [functools.partial(receive, block)] if k == 0 else []
        return arrive + [
            functools.partial(rotate_slabs, k, block, half, i)
            for half in range(2)
            for i in range(0, BLOCK // SLAB, SLAB)
        ]

    def multiply(k, block):
        target = result if k == 2 else current
        parts = [
            functools.partial(multiply_part, k, SPLIT, block, part, target, mixed, weight)
            for part in range(4)
        ]
        return parts + [leaving[block].start] if k == 2 else parts

    pipeline(3, rotate, multiply)
    for copy in leaving:
        copy.wait()


def outer_levels(*operands):
    return pl.pallas_call(
        outer_kernel,
        in_specs=[VMEM] * len(operands),
        out_specs=HBM,
        out_shape=jax.ShapeDtypeStruct((ROWS, WIDTH), jnp.bfloat16),
        scratch_shapes=[
            pltpu.VMEM((ROWS, WIDTH), jnp.float32),
            pltpu.VMEM((ROWS // 2, 2 * WIDTH), jnp.bfloat16),
            pltpu.VMEM((ROWS, WIDTH), jnp.bfloat16),
            DMA((2,)),
        ],
        compiler_params=pltpu.CompilerParams(vmem_limit_bytes=32 << 20),
        cost_estimate=pl.CostEstimate(flops=3 << 30, bytes_accessed=8 << 20, transcendentals=0),
        name="levels10to12",
    )(*operands)


def exchange(blocks):
    return lax.all_to_all(blocks, AXES, 0, 0, tiled=True)


def on_device(signal, box_phase, node_phase, local_interp, across_x, across_y):
    own = box_phase[:, 0]
    moved = exchange(first_levels(signal[0, 0], own, node_phase, local_interp))
    last_cos, last_sin, own_cos, own_sin, local, x_weight, y_weight = prep(
        own, node_phase, local_interp, across_x, across_y
    )
    inner = inner_levels(moved, own_cos, own_sin, x_weight, y_weight)
    return outer_levels(exchange(inner), last_cos, last_sin, local)[None, None]


def solution(mesh):
    return jax.shard_map(
        on_device,
        mesh=mesh,
        in_specs=(P("sx", "sy", None, None), P(None, "sx", "sy", None), P(), P(), P(), P()),
        out_specs=P("sx", "sy", None, None),
        check_vma=False,
    )
```

```python
import functools

import jax
import jax.numpy as jnp
from jax import lax
from jax.experimental import pallas as pl
from jax.experimental.pallas import tpu as pltpu
from jax.sharding import PartitionSpec as P

AXES = ("sx", "sy")
ROWS = 1024
NODES = 256
WIDTH = 512
BOXES = 128
SLAB = 8
CHUNK = 64
HALF = ROWS // 2
STRIP = 128
CODE = 38.0
MESSAGE = 48
DATA = 32
FIRST = 3
INNER = 7
LAST = FIRST + INNER
BLOCK = 256
BOX_BITS = (4, 0, 5, 1, 6, 2, 3)
SECOND = (0, 1, 0, 1, 0, 1, 1)
SPLITS = (6, 6, 6, 5, 5, 5, 5)
SPLIT = 6

SIN = (9.99999242e-01, -1.66656797e-01, 8.31322541e-03, -1.85234428e-04)
COS = (0.99999325, -0.49991211, 0.04148738, -0.00127111)


def horner(coefficients, x):
    total = coefficients[-1] * x + coefficients[-2]
    for factor in coefficients[-3::-1]:
        total = total * x + factor
    return total


def cos_sin(angle):
    half = angle * 0.5
    square = half * half
    sine = half * horner(SIN, square)
    cosine = horner(COS, square)
    double = sine + sine
    return 1.0 - double * sine, double * cosine


def pair_slabs(bit, half, split, block):
    return [
        slab
        for slab in range(BOXES)
        if slab >> bit & 1 == half and slab >> split & 1 == block
    ]


def runs(slabs):
    found = []
    for i, slab in enumerate(slabs):
        if found and found[-1][1] + found[-1][2] == slab * SLAB:
            found[-1][2] += SLAB
        else:
            found.append([i * SLAB, slab * SLAB, SLAB])
    return found


def load_slabs(ref, slabs, columns):
    parts = [ref[r : r + n, columns] for _, r, n in runs(slabs)]
    return parts[0] if len(parts) == 1 else jnp.concatenate(parts, axis=0)


def interleave(major, minor):
    done = 0
    for i, step in enumerate(major):
        step()
        upto = len(minor) * (i + 1) // len(major)
        for other in minor[done:upto]:
            other()
        done = upto
    for other in minor[done:]:
        other()


def pipeline(levels, rotate, multiply, apart=()):
    stages = [(k, block) for k in range(levels) for block in range(2)]
    ready = rotate(*stages[0])
    for i, stage in enumerate(stages):
        if i == 0 or stage in apart:
            interleave(ready, [])
        after = stages[i + 1] if i + 1 < len(stages) else None
        ready = rotate(*after) if after else []
        interleave(multiply(*stage), [] if after in apart else ready)


RE = slice(0, NODES)
IM = slice(NODES, WIDTH)


VMEM = pl.BlockSpec(memory_space=pltpu.VMEM)
HBM = pl.BlockSpec(memory_space=pltpu.HBM)
DMA = pltpu.SemaphoreType.DMA


def fill_weight(weight, interp):
    for child in range(2):
        for source in range(2):
            r, c = source * WIDTH, child * WIDTH
            real, imag = interp[child, source, 0], interp[child, source, 1]
            weight[r : r + NODES, c : c + NODES] = real
            weight[r : r + NODES, c + NODES : c + WIDTH] = imag
            weight[r + NODES : r + WIDTH, c : c + NODES] = -imag
            weight[r + NODES : r + WIDTH, c + NODES : c + WIDTH] = real


def product(mixed, block, part, weight):
    return jnp.dot(
        mixed[block * BLOCK : (block + 1) * BLOCK],
        weight[:, part * NODES : (part + 1) * NODES],
        preferred_element_type=jnp.float32,
    )


def strip(j):
    return slice(j * STRIP, (j + 1) * STRIP)


def rotate_into(mixed, rows, half, re, im, c, s):
    left = half * WIDTH
    mixed[rows, left : left + NODES] = (re * c - im * s).astype(jnp.bfloat16)
    mixed[rows, left + NODES : left + WIDTH] = (re * s + im * c).astype(jnp.bfloat16)


def first_kernel(
    data_hbm, box_ref, node_hbm, interp_hbm, out_hbm,
    data, nodes, interp, weight, cosines, sines, current, mixed, messages, sems,
):
    copies = [
        pltpu.make_async_copy(node_hbm.at[0], nodes.at[0], sems.at[0]),
        pltpu.make_async_copy(interp_hbm, interp, sems.at[1]),
        pltpu.make_async_copy(data_hbm, data, sems.at[2]),
    ] + [pltpu.make_async_copy(node_hbm.at[k], nodes.at[k], sems.at[2 + k]) for k in (1, 2)]
    for copy in copies:
        copy.start()
    boxes = [cos_sin(box_ref[k]) for k in range(FIRST)]
    phases = [
        box_ref[min(FIRST + k, LAST - 1)][:, strip(j)] for j in range(2) for k in range(SLAB)
    ]
    code = jnp.exp2(jnp.concatenate(phases, axis=0) * CODE).astype(jnp.bfloat16)
    messages[:, DATA:, :] = jnp.broadcast_to(code[None], (BOXES, 2 * SLAB, STRIP))

    def turn(k, rows, columns):
        node_cos, node_sin = cos_sin(nodes[k, rows, columns])
        box_cos, box_sin = boxes[k][0][:, columns], boxes[k][1][:, columns]
        return node_cos * box_cos - node_sin * box_sin, node_sin * box_cos + node_cos * box_sin

    copies[0].wait()
    for first in range(0, ROWS, CHUNK):
        for j in range(2):
            rows = slice(first, first + CHUNK)
            cosines[rows, strip(j)], sines[rows, strip(j)] = turn(0, rows, strip(j))
    copies[1].wait()
    fill_weight(weight, interp)
    copies[2].wait()

    def swap(bit, zero, one):
        distance = 1 << bit
        at_zero = lax.broadcasted_iota(jnp.int32, zero.shape, 1) & distance == 0
        return (
            jnp.where(at_zero, zero, pltpu.roll(one, distance, 1)),
            jnp.where(at_zero, pltpu.roll(zero, SLAB - distance, 1), one),
        )

    def rotate_rows(k, block, i, j):
        sides = []
        for side in range(2):
            first = block * HALF + side * BLOCK + i * CHUNK
            rows = slice(first, first + CHUNK)
            if k:
                c, s = turn(k, rows, strip(j))
            else:
                c, s = cosines[rows, strip(j)], sines[rows, strip(j)]
            source = current if k else data
            re = source[rows, strip(j)].astype(jnp.float32)
            im = source[rows, strip(2 + j)].astype(jnp.float32)
            sides.append((re * c - im * s, re * s + im * c))
        at = block * BLOCK + i * CHUNK
        for part in range(2):
            pair = [side[part].reshape(CHUNK // SLAB, SLAB, STRIP) for side in sides]
            for half, rows in enumerate(swap(k, *pair)):
                mixed[at : at + CHUNK, strip(4 * half + 2 * part + j)] = rows.reshape(
                    CHUNK, STRIP
                ).astype(jnp.bfloat16)

    def rotate(k, block):
        if k and block == 0:
            copies[2 + k].wait()
        return [
            functools.partial(rotate_rows, k, block, i, j)
            for i in range(BLOCK // CHUNK)
            for j in range(2)
        ]

    def multiply_part(k, block, part):
        pair = [
            product(mixed, block, 2 * child + part, weight).reshape(
                BLOCK // SLAB, SLAB, NODES
            )
            for child in range(2)
        ]
        for side, rows in enumerate(swap(k, *pair)):
            if k < FIRST - 1:
                first = block * HALF + side * BLOCK
                current[first : first + BLOCK, (RE, IM)[part]] = rows.reshape(BLOCK, NODES)
            else:
                first = (block * HALF + side * BLOCK) // SLAB
                both = jnp.concatenate([rows[:, :, strip(0)], rows[:, :, strip(1)]], axis=1)
                messages[
                    first : first + BLOCK // SLAB, 2 * SLAB * part : 2 * SLAB * (part + 1), :
                ] = both.astype(jnp.bfloat16)

    def multiply(k, block):
        return [functools.partial(multiply_part, k, block, part) for part in range(2)] + [
            functools.partial(leave, k, block)
        ]

    leaving = [
        pltpu.make_async_copy(
            messages.at[pl.ds(block * CHUNK, CHUNK)],
            out_hbm.at[pl.ds(block * CHUNK, CHUNK)],
            sems.at[5 + block],
        )
        for block in range(2)
    ]

    def leave(k, block):
        if k == FIRST - 1:
            leaving[block].start()

    pipeline(FIRST, rotate, multiply)
    for copy in leaving:
        copy.wait()


def first_levels(data, box_phase, node_phase, interp):
    return pl.pallas_call(
        first_kernel,
        in_specs=[HBM, VMEM, HBM, HBM],
        out_specs=HBM,
        out_shape=jax.ShapeDtypeStruct((BOXES, MESSAGE, STRIP), jnp.bfloat16),
        scratch_shapes=[
            pltpu.VMEM((ROWS, WIDTH), jnp.bfloat16),
            pltpu.VMEM((FIRST, ROWS, NODES), jnp.float32),
            pltpu.VMEM((2, 2, 2, NODES, NODES), jnp.bfloat16),
            pltpu.VMEM((2 * WIDTH, 2 * WIDTH), jnp.bfloat16),
            pltpu.VMEM((ROWS, NODES), jnp.float32),
            pltpu.VMEM((ROWS, NODES), jnp.float32),
            pltpu.VMEM((ROWS, WIDTH), jnp.float32),
            pltpu.VMEM((ROWS // 2, 2 * WIDTH), jnp.bfloat16),
            pltpu.VMEM((BOXES, MESSAGE, STRIP), jnp.bfloat16),
            DMA((7,)),
        ],
        compiler_params=pltpu.CompilerParams(vmem_limit_bytes=58 << 20),
        cost_estimate=pl.CostEstimate(flops=3 << 30, bytes_accessed=8 << 20, transcendentals=0),
        name="levels0to2",
    )(data, box_phase, node_phase, interp)


def prep_kernel(
    box_ref, node_hbm, local_hbm, x_hbm, y_hbm,
    cos_ref, sin_ref, own_cos, own_sin, local_weight, x_weight, y_weight,
    own, nodes, interps, sems,
):
    me = lax.axis_index("sx") * lax.axis_size("sy") + lax.axis_index("sy")
    rows = pl.ds(pl.multiple_of(me * SLAB, SLAB), SLAB)
    copies = [
        pltpu.make_async_copy(node_hbm.at[pl.ds(FIRST, INNER), rows, :], own, sems.at[0]),
    ] + [pltpu.make_async_copy(node_hbm.at[LAST + k], nodes.at[k], sems.at[1 + k]) for k in range(3)]
    copies += [
        pltpu.make_async_copy(hbm, interps.at[k], sems.at[4 + k])
        for k, hbm in enumerate((x_hbm, y_hbm, local_hbm))
    ]
    for copy in copies:
        copy.start()
    copies[0].wait()
    own_cos[...], own_sin[...] = cos_sin(own[...])
    for k, weight in enumerate((x_weight, y_weight, local_weight)):
        copies[4 + k].wait()
        fill_weight(weight, interps.at[k])
    for k in range(3):
        copies[1 + k].wait()
        box_cos, box_sin = cos_sin(box_ref[LAST + k])
        for half in range(2):
            for block in range(2):
                slabs = pair_slabs(k, half, SPLIT, block)
                for i in range(0, len(slabs), SLAB):
                    angles = load_slabs(nodes.at[k], slabs[i : i + SLAB], slice(None))
                    node_cos, node_sin = cos_sin(angles)
                    at = half * HALF + block * BLOCK + i * SLAB
                    cosine = node_cos * box_cos - node_sin * box_sin
                    sine = node_sin * box_cos + node_cos * box_sin
                    cos_ref[k, at : at + CHUNK, :] = cosine.astype(jnp.bfloat16)
                    sin_ref[k, at : at + CHUNK, :] = sine.astype(jnp.bfloat16)


def prep(box_phase, node_phase, *interps):
    weight = jax.ShapeDtypeStruct((2 * WIDTH, 2 * WIDTH), jnp.bfloat16)
    table = jax.ShapeDtypeStruct((3, ROWS, NODES), jnp.bfloat16)
    own = jax.ShapeDtypeStruct((INNER, SLAB, NODES), jnp.float32)
    return pl.pallas_call(
        prep_kernel,
        in_specs=[VMEM] + [HBM] * 4,
        out_specs=[VMEM] * 7,
        out_shape=[table, table, own, own, weight, weight, weight],
        scratch_shapes=[
            pltpu.VMEM((INNER, SLAB, NODES), jnp.float32),
            pltpu.VMEM((3, ROWS, NODES), jnp.float32),
            pltpu.VMEM((3, 2, 2, 2, NODES, NODES), jnp.bfloat16),
            DMA((7,)),
        ],
        compiler_params=pltpu.CompilerParams(vmem_limit_bytes=52 << 20),
        cost_estimate=pl.CostEstimate(flops=60_000_000, bytes_accessed=7 << 20, transcendentals=0),
        name="prep",
    )(box_phase, node_phase, *interps)


def multiply_part(bit, split, block, part, target, mixed, weight):
    total = product(mixed, block, part, weight)
    for at, r, n in runs(pair_slabs(bit, part >> 1, split, block)):
        target[r : r + n, (RE, IM)[part & 1]] = total[at : at + n].astype(target.dtype)


def inner_kernel(
    data_ref, own_cos, own_sin, x_hbm, y_hbm, out_ref,
    current, mixed, box_cos, box_sin, weights, sems,
):
    copies = [
        pltpu.make_async_copy(hbm, weights.at[i], sems.at[i]) for i, hbm in enumerate((x_hbm, y_hbm))
    ]
    copies[0].start()

    def receive(block, part):
        boxes = slice(block * CHUNK, (block + 1) * CHUNK)
        if part == 2:
            phase = jnp.log2(data_ref[boxes, DATA:, :].astype(jnp.float32)) * (1.0 / CODE)
            box_cos[boxes], box_sin[boxes] = cos_sin(phase)
        else:
            pair = data_ref[boxes, 2 * SLAB * part : 2 * SLAB * (part + 1), :].astype(jnp.float32)
            for i in range(2):
                piece = pair[:, i * SLAB : (i + 1) * SLAB, :]
                current[block * HALF : (block + 1) * HALF, strip(2 * part + i)] = piece.reshape(
                    HALF, STRIP
                )

    def rotate_slabs(k, block, half, i, j):
        slabs = pair_slabs(BOX_BITS[k], half, SPLITS[k], block)[i : i + SLAB]
        node_cos, node_sin = own_cos[k, :, strip(j)], own_sin[k, :, strip(j)]
        at = slice(SLAB * j + k, SLAB * j + k + 1)
        re_parts, im_parts = [], []
        for slab in slabs:
            c, s = box_cos[slab, at, :], box_sin[slab, at, :]
            cosine = c * node_cos - s * node_sin
            sine = s * node_cos + c * node_sin
            rows = slice(slab * SLAB, (slab + 1) * SLAB)
            re, im = current[rows, strip(j)], current[rows, strip(2 + j)]
            re_parts.append(re * cosine - im * sine)
            im_parts.append(re * sine + im * cosine)
        first = block * BLOCK + i * SLAB
        to = slice(first, first + CHUNK)
        for parts, column in ((re_parts, j), (im_parts, 2 + j)):
            joined = jnp.concatenate(parts, axis=0).astype(jnp.bfloat16)
            mixed[to, strip(4 * half + column)] = joined

    def rotate(k, block):
        steps = [
            functools.partial(rotate_slabs, k, block, half, i, j)
            for half in range(2)
            for i in range(0, BLOCK // SLAB, SLAB)
            for j in range(2)
        ]
        if k:
            return steps
        steps = [functools.partial(receive, block, part) for part in range(3)] + steps
        return steps + [copies[1].start] + rotate(0, 1) if block == 0 else steps

    def multiply(k, block):
        target = out_ref if k == INNER - 1 else current
        if k < 2 and block == 0:
            copies[k].wait()
        return [
            functools.partial(
                multiply_part, BOX_BITS[k], SPLITS[k], block, part, target, mixed,
                weights.at[SECOND[k]],
            )
            for part in range(4)
        ]

    def rotate_later(k, block):
        return [] if (k, block) == (0, 1) else rotate(k, block)

    pipeline(INNER, rotate_later, multiply, apart=[(3, 0)])


def inner_levels(*operands):
    return pl.pallas_call(
        inner_kernel,
        in_specs=[VMEM] * 3 + [HBM] * 2,
        out_specs=VMEM,
        out_shape=jax.ShapeDtypeStruct((ROWS, WIDTH), jnp.bfloat16),
        scratch_shapes=[
            pltpu.VMEM((ROWS, WIDTH), jnp.float32),
            pltpu.VMEM((ROWS // 2, 2 * WIDTH), jnp.bfloat16),
            pltpu.VMEM((BOXES, 2 * SLAB, STRIP), jnp.float32),
            pltpu.VMEM((BOXES, 2 * SLAB, STRIP), jnp.float32),
            pltpu.VMEM((2, 2 * WIDTH, 2 * WIDTH), jnp.bfloat16),
            DMA((2,)),
        ],
        compiler_params=pltpu.CompilerParams(vmem_limit_bytes=50 << 20),
        cost_estimate=pl.CostEstimate(flops=7 << 30, bytes_accessed=8 << 20, transcendentals=0),
        name="levels3to9",
    )(*operands)


def outer_kernel(
    data_ref, cos_ref, sin_ref, weight, out_hbm, current, mixed, result, sems
):
    def receive(block):
        rows = slice(block * HALF, (block + 1) * HALF)
        current[rows] = data_ref[rows].astype(jnp.float32)

    leaving = [
        pltpu.make_async_copy(
            result.at[pl.ds(block * HALF, HALF)],
            out_hbm.at[pl.ds(block * HALF, HALF)],
            sems.at[block],
        )
        for block in range(2)
    ]

    def rotate_slabs(k, block, half, i):
        slabs = pair_slabs(k, half, SPLIT, block)[i : i + SLAB]
        first = block * BLOCK + i * SLAB
        at = half * HALF + first
        rotate_into(
            mixed,
            slice(first, first + CHUNK),
            half,
            load_slabs(current, slabs, RE),
            load_slabs(current, slabs, IM),
            cos_ref[k, at : at + CHUNK, :].astype(jnp.float32),
            sin_ref[k, at : at + CHUNK, :].astype(jnp.float32),
        )

    def rotate(k, block):
        arrive = [functools.partial(receive, block)] if k == 0 else []
        return arrive + [
            functools.partial(rotate_slabs, k, block, half, i)
            for half in range(2)
            for i in range(0, BLOCK // SLAB, SLAB)
        ]

    def multiply(k, block):
        target = result if k == 2 else current
        parts = [
            functools.partial(multiply_part, k, SPLIT, block, part, target, mixed, weight)
            for part in range(4)
        ]
        return parts + [leaving[block].start] if k == 2 else parts

    pipeline(3, rotate, multiply)
    for copy in leaving:
        copy.wait()


def outer_levels(*operands):
    return pl.pallas_call(
        outer_kernel,
        in_specs=[VMEM] * len(operands),
        out_specs=HBM,
        out_shape=jax.ShapeDtypeStruct((ROWS, WIDTH), jnp.bfloat16),
        scratch_shapes=[
            pltpu.VMEM((ROWS, WIDTH), jnp.float32),
            pltpu.VMEM((ROWS // 2, 2 * WIDTH), jnp.bfloat16),
            pltpu.VMEM((ROWS, WIDTH), jnp.bfloat16),
            DMA((2,)),
        ],
        compiler_params=pltpu.CompilerParams(vmem_limit_bytes=32 << 20),
        cost_estimate=pl.CostEstimate(flops=3 << 30, bytes_accessed=8 << 20, transcendentals=0),
        name="levels10to12",
    )(*operands)


def exchange(blocks):
    return lax.all_to_all(blocks, AXES, 0, 0, tiled=True)


def on_device(signal, box_phase, node_phase, local_interp, across_x, across_y):
    own = box_phase[:, 0]
    moved = exchange(first_levels(signal[0, 0], own, node_phase, local_interp))
    last_cos, last_sin, own_cos, own_sin, local, x_weight, y_weight = prep(
        own, node_phase, local_interp, across_x, across_y
    )
    inner = inner_levels(moved, own_cos, own_sin, x_weight, y_weight)
    return outer_levels(exchange(inner), last_cos, last_sin, local)[None, None]


def solution(mesh):
    return jax.shard_map(
        on_device,
        mesh=mesh,
        in_specs=(P("sx", "sy", None, None), P(None, "sx", "sy", None), P(), P(), P(), P()),
        out_specs=P("sx", "sy", None, None),
        check_vma=False,
    )
```

```python
import functools

import jax
import jax.numpy as jnp
from jax import lax
from jax.experimental import pallas as pl
from jax.experimental.pallas import tpu as pltpu
from jax.sharding import PartitionSpec as P

AXES = ("sx", "sy")
ROWS = 1024
NODES = 256
WIDTH = 512
BOXES = 128
SLAB = 8
CHUNK = 64
HALF = ROWS // 2
STRIP = 128
CODE = 38.0
MESSAGE = 48
DATA = 32
FIRST = 1
INNER = 9
LAST = FIRST + INNER
WITHIN = 2
BLOCK = 256
BOX_BITS = (4, 0, 5, 1, 6, 2, 3)
SECOND = (0, 1, 0, 1, 0, 1, 1)
SPLITS = (6, 6, 6, 5, 5, 5, 5)
SPLIT = 6

SIN = (9.99999242e-01, -1.66656797e-01, 8.31322541e-03, -1.85234428e-04)
COS = (0.99999325, -0.49991211, 0.04148738, -0.00127111)


def horner(coefficients, x):
    total = coefficients[-1] * x + coefficients[-2]
    for factor in coefficients[-3::-1]:
        total = total * x + factor
    return total


def cos_sin(angle):
    half = angle * 0.5
    square = half * half
    sine = half * horner(SIN, square)
    cosine = horner(COS, square)
    double = sine + sine
    return 1.0 - double * sine, double * cosine


def pair_slabs(bit, half, split, block):
    return [
        slab
        for slab in range(BOXES)
        if slab >> bit & 1 == half and slab >> split & 1 == block
    ]


def runs(slabs):
    found = []
    for i, slab in enumerate(slabs):
        if found and found[-1][1] + found[-1][2] == slab * SLAB:
            found[-1][2] += SLAB
        else:
            found.append([i * SLAB, slab * SLAB, SLAB])
    return found


def load_slabs(ref, slabs, columns):
    parts = [ref[r : r + n, columns] for _, r, n in runs(slabs)]
    return parts[0] if len(parts) == 1 else jnp.concatenate(parts, axis=0)


def interleave(major, minor):
    done = 0
    for i, step in enumerate(major):
        step()
        upto = len(minor) * (i + 1) // len(major)
        for other in minor[done:upto]:
            other()
        done = upto
    for other in minor[done:]:
        other()


def pipeline(levels, rotate, multiply, apart=()):
    stages = [(k, block) for k in range(levels) for block in range(2)]
    ready = rotate(*stages[0])
    for i, stage in enumerate(stages):
        if i == 0 or stage in apart:
            interleave(ready, [])
        after = stages[i + 1] if i + 1 < len(stages) else None
        ready = rotate(*after) if after else []
        interleave(multiply(*stage), [] if after in apart else ready)


RE = slice(0, NODES)
IM = slice(NODES, WIDTH)


VMEM = pl.BlockSpec(memory_space=pltpu.VMEM)
HBM = pl.BlockSpec(memory_space=pltpu.HBM)
DMA = pltpu.SemaphoreType.DMA


def fill_weight(weight, interp):
    for child in range(2):
        for source in range(2):
            r, c = source * WIDTH, child * WIDTH
            real, imag = interp[child, source, 0], interp[child, source, 1]
            weight[r : r + NODES, c : c + NODES] = real
            weight[r : r + NODES, c + NODES : c + WIDTH] = imag
            weight[r + NODES : r + WIDTH, c : c + NODES] = -imag
            weight[r + NODES : r + WIDTH, c + NODES : c + WIDTH] = real


def product(mixed, block, part, weight):
    return jnp.dot(
        mixed[block * BLOCK : (block + 1) * BLOCK],
        weight[:, part * NODES : (part + 1) * NODES],
        preferred_element_type=jnp.float32,
    )


def strip(j):
    return slice(j * STRIP, (j + 1) * STRIP)


def rotate_into(mixed, rows, half, re, im, c, s):
    left = half * WIDTH
    mixed[rows, left : left + NODES] = (re * c - im * s).astype(jnp.bfloat16)
    mixed[rows, left + NODES : left + WIDTH] = (re * s + im * c).astype(jnp.bfloat16)


def swap(bit, zero, one):
    distance = 1 << bit
    at_zero = lax.broadcasted_iota(jnp.int32, zero.shape, 1) & distance == 0
    return (
        jnp.where(at_zero, zero, pltpu.roll(one, distance, 1)),
        jnp.where(at_zero, pltpu.roll(zero, SLAB - distance, 1), one),
    )


def mix_within(bit, block, i, j, sides, mixed):
    at = block * BLOCK + i * CHUNK
    for part in range(2):
        pair = [side[part].reshape(CHUNK // SLAB, SLAB, STRIP) for side in sides]
        for half, rows in enumerate(swap(bit, *pair)):
            mixed[at : at + CHUNK, strip(4 * half + 2 * part + j)] = rows.reshape(
                CHUNK, STRIP
            ).astype(jnp.bfloat16)


def multiply_within(bit, block, part, target, mixed, weight):
    pair = [
        product(mixed, block, 2 * child + part, weight).reshape(BLOCK // SLAB, SLAB, NODES)
        for child in range(2)
    ]
    for side, rows in enumerate(swap(bit, *pair)):
        first = block * HALF + side * BLOCK
        target[first : first + BLOCK, (RE, IM)[part]] = rows.reshape(BLOCK, NODES)


def first_kernel(
    data_hbm, box_ref, node_hbm, interp_hbm, out_hbm,
    data, nodes, interp, weight, cosines, sines, current, mixed, messages, sems,
):
    copies = [
        pltpu.make_async_copy(node_hbm.at[0], nodes, sems.at[0]),
        pltpu.make_async_copy(interp_hbm, interp, sems.at[1]),
        pltpu.make_async_copy(data_hbm, data, sems.at[2]),
    ]
    for copy in copies:
        copy.start()
    box_cos, box_sin = cos_sin(box_ref[0])
    next_cos, next_sin = cos_sin(box_ref[1])
    phases = [box_ref[FIRST + 1 + k][:, strip(j)] for j in range(2) for k in range(SLAB)]
    code = jnp.exp2(jnp.concatenate(phases, axis=0) * CODE).astype(jnp.bfloat16)
    messages[:, DATA:, :] = jnp.broadcast_to(code[None], (BOXES, 2 * SLAB, STRIP))
    copies[0].wait()
    for first in range(0, ROWS, CHUNK):
        for j in range(2):
            rows, columns = slice(first, first + CHUNK), strip(j)
            node_cos, node_sin = cos_sin(nodes[rows, columns])
            c, s = box_cos[:, columns], box_sin[:, columns]
            cosines[rows, columns] = node_cos * c - node_sin * s
            sines[rows, columns] = node_sin * c + node_cos * s
    copies[1].wait()
    fill_weight(weight, interp)
    copies[2].wait()

    def rotate_rows(block, i, j):
        sides = []
        for side in range(2):
            first = block * HALF + side * BLOCK + i * CHUNK
            rows = slice(first, first + CHUNK)
            c, s = cosines[rows, strip(j)], sines[rows, strip(j)]
            re = data[rows, strip(j)].astype(jnp.float32)
            im = data[rows, strip(2 + j)].astype(jnp.float32)
            sides.append((re * c - im * s, re * s + im * c))
        mix_within(0, block, i, j, sides, mixed)

    def rotate(k, block):
        return [
            functools.partial(rotate_rows, block, i, j)
            for i in range(BLOCK // CHUNK)
            for j in range(2)
        ]

    def pack(block, i):
        first = block * HALF + i * CHUNK
        rows, slabs = slice(first, first + CHUNK), slice(first // SLAB, (first + CHUNK) // SLAB)
        turned = []
        for j in range(2):
            c, s = next_cos[:, strip(j)], next_sin[:, strip(j)]
            re, im = current[rows, strip(j)], current[rows, strip(2 + j)]
            turned.append((re * c - im * s, re * s + im * c))
        for part in range(2):
            pair = [turned[j][part].reshape(CHUNK // SLAB, SLAB, STRIP) for j in range(2)]
            messages[slabs, 2 * SLAB * part : 2 * SLAB * (part + 1), :] = jnp.concatenate(
                pair, axis=1
            ).astype(jnp.bfloat16)

    leaving = [
        pltpu.make_async_copy(
            messages.at[pl.ds(block * CHUNK, CHUNK)],
            out_hbm.at[pl.ds(block * CHUNK, CHUNK)],
            sems.at[3 + block],
        )
        for block in range(2)
    ]

    def multiply(k, block):
        steps = [
            functools.partial(multiply_within, 0, block, part, current, mixed, weight)
            for part in range(2)
        ]
        steps += [functools.partial(pack, block, i) for i in range(HALF // CHUNK)]
        return steps + [leaving[block].start]

    pipeline(1, rotate, multiply)
    for copy in leaving:
        copy.wait()


def first_levels(data, box_phase, node_phase, interp):
    return pl.pallas_call(
        first_kernel,
        in_specs=[HBM, VMEM, HBM, HBM],
        out_specs=HBM,
        out_shape=jax.ShapeDtypeStruct((BOXES, MESSAGE, STRIP), jnp.bfloat16),
        scratch_shapes=[
            pltpu.VMEM((ROWS, WIDTH), jnp.bfloat16),
            pltpu.VMEM((ROWS, NODES), jnp.float32),
            pltpu.VMEM((2, 2, 2, NODES, NODES), jnp.bfloat16),
            pltpu.VMEM((2 * WIDTH, 2 * WIDTH), jnp.bfloat16),
            pltpu.VMEM((ROWS, NODES), jnp.float32),
            pltpu.VMEM((ROWS, NODES), jnp.float32),
            pltpu.VMEM((ROWS, WIDTH), jnp.float32),
            pltpu.VMEM((ROWS // 2, 2 * WIDTH), jnp.bfloat16),
            pltpu.VMEM((BOXES, MESSAGE, STRIP), jnp.bfloat16),
            DMA((5,)),
        ],
        compiler_params=pltpu.CompilerParams(vmem_limit_bytes=58 << 20),
        cost_estimate=pl.CostEstimate(flops=1 << 30, bytes_accessed=8 << 20, transcendentals=0),
        name="level0",
    )(data, box_phase, node_phase, interp)


def prep_kernel(
    box_ref, node_hbm, local_hbm, x_hbm, y_hbm,
    cos_ref, sin_ref, own_cos, own_sin, local_weight, inner_weight, x_weight, y_weight,
    own, nodes, interps, sems,
):
    me = lax.axis_index("sx") * lax.axis_size("sy") + lax.axis_index("sy")
    rows = pl.ds(pl.multiple_of(me * SLAB, SLAB), SLAB)
    copies = [
        pltpu.make_async_copy(node_hbm.at[pl.ds(FIRST, INNER), rows, :], own, sems.at[0]),
    ] + [pltpu.make_async_copy(node_hbm.at[LAST + k], nodes.at[k], sems.at[1 + k]) for k in range(3)]
    copies += [
        pltpu.make_async_copy(hbm, interps.at[k], sems.at[4 + k])
        for k, hbm in enumerate((x_hbm, y_hbm, local_hbm))
    ]
    for copy in copies:
        copy.start()
    copies[0].wait()
    own_cos[...], own_sin[...] = cos_sin(own[...])
    for k, weight in enumerate((x_weight, y_weight, local_weight)):
        copies[4 + k].wait()
        fill_weight(weight, interps.at[k])
    fill_weight(inner_weight, interps.at[2])
    for k in range(3):
        copies[1 + k].wait()
        box_cos, box_sin = cos_sin(box_ref[LAST + k])
        for half in range(2):
            for block in range(2):
                slabs = pair_slabs(k, half, SPLIT, block)
                for i in range(0, len(slabs), SLAB):
                    angles = load_slabs(nodes.at[k], slabs[i : i + SLAB], slice(None))
                    node_cos, node_sin = cos_sin(angles)
                    at = half * HALF + block * BLOCK + i * SLAB
                    cosine = node_cos * box_cos - node_sin * box_sin
                    sine = node_sin * box_cos + node_cos * box_sin
                    cos_ref[k, at : at + CHUNK, :] = cosine.astype(jnp.bfloat16)
                    sin_ref[k, at : at + CHUNK, :] = sine.astype(jnp.bfloat16)


def prep(box_phase, node_phase, *interps):
    weight = jax.ShapeDtypeStruct((2 * WIDTH, 2 * WIDTH), jnp.bfloat16)
    table = jax.ShapeDtypeStruct((3, ROWS, NODES), jnp.bfloat16)
    own = jax.ShapeDtypeStruct((INNER, SLAB, NODES), jnp.float32)
    return pl.pallas_call(
        prep_kernel,
        in_specs=[VMEM] + [HBM] * 4,
        out_specs=[VMEM] * 8,
        out_shape=[table, table, own, own, weight, weight, weight, weight],
        scratch_shapes=[
            pltpu.VMEM((INNER, SLAB, NODES), jnp.float32),
            pltpu.VMEM((3, ROWS, NODES), jnp.float32),
            pltpu.VMEM((3, 2, 2, 2, NODES, NODES), jnp.bfloat16),
            DMA((7,)),
        ],
        compiler_params=pltpu.CompilerParams(vmem_limit_bytes=52 << 20),
        cost_estimate=pl.CostEstimate(flops=60_000_000, bytes_accessed=7 << 20, transcendentals=0),
        name="prep",
    )(box_phase, node_phase, *interps)


def multiply_part(bit, split, block, part, target, mixed, weight):
    total = product(mixed, block, part, weight)
    for at, r, n in runs(pair_slabs(bit, part >> 1, split, block)):
        target[r : r + n, (RE, IM)[part & 1]] = total[at : at + n].astype(target.dtype)


def inner_kernel(
    data_ref, own_cos, own_sin, local_hbm, x_hbm, y_hbm, out_ref,
    current, mixed, box_cos, box_sin, weights, sems,
):
    copies = [
        pltpu.make_async_copy(hbm, weights.at[i], sems.at[i])
        for i, hbm in enumerate((local_hbm, x_hbm, y_hbm))
    ]
    copies[0].start()

    def receive(block, part):
        boxes = slice(block * CHUNK, (block + 1) * CHUNK)
        if part == 2:
            phase = jnp.log2(data_ref[boxes, DATA:, :].astype(jnp.float32)) * (1.0 / CODE)
            box_cos[boxes], box_sin[boxes] = cos_sin(phase)
        else:
            pair = data_ref[boxes, 2 * SLAB * part : 2 * SLAB * (part + 1), :].astype(jnp.float32)
            for i in range(2):
                piece = pair[:, i * SLAB : (i + 1) * SLAB, :]
                current[block * HALF : (block + 1) * HALF, strip(2 * part + i)] = piece.reshape(
                    HALF, STRIP
                )

    def turn(k, j, slabs):
        node_cos, node_sin = own_cos[k, :, strip(j)], own_sin[k, :, strip(j)]
        at = slice(SLAB * j + k - 1, SLAB * j + k)
        re_parts, im_parts = [], []
        for slab in slabs:
            if k:
                c, s = box_cos[slab, at, :], box_sin[slab, at, :]
                cosine = c * node_cos - s * node_sin
                sine = s * node_cos + c * node_sin
            else:
                cosine, sine = node_cos, node_sin
            rows = slice(slab * SLAB, (slab + 1) * SLAB)
            re, im = current[rows, strip(j)], current[rows, strip(2 + j)]
            re_parts.append(re * cosine - im * sine)
            im_parts.append(re * sine + im * cosine)
        return jnp.concatenate(re_parts, axis=0), jnp.concatenate(im_parts, axis=0)

    def rotate_within(k, block, i, j):
        first = (block * HALF + i * CHUNK) // SLAB
        sides = [
            turn(k, j, range(first + side, first + side + SLAB)) for side in (0, BLOCK // SLAB)
        ]
        mix_within(1 + k, block, i, j, sides, mixed)

    def rotate_slabs(k, block, half, i, j):
        slabs = pair_slabs(BOX_BITS[k - WITHIN], half, SPLITS[k - WITHIN], block)[i : i + SLAB]
        first = block * BLOCK + i * SLAB
        to = slice(first, first + CHUNK)
        for part, turned in enumerate(turn(k, j, slabs)):
            mixed[to, strip(4 * half + 2 * part + j)] = turned.astype(jnp.bfloat16)

    def rotate(k, block):
        if k >= WITHIN:
            return [
                functools.partial(rotate_slabs, k, block, half, i, j)
                for half in range(2)
                for i in range(0, BLOCK // SLAB, SLAB)
                for j in range(2)
            ]
        steps = [
            functools.partial(rotate_within, k, block, i, j)
            for i in range(BLOCK // CHUNK)
            for j in range(2)
        ]
        if k:
            return steps
        steps = [functools.partial(receive, block, part) for part in range(3)] + steps
        return steps + rotate(0, 1) if block == 0 else steps

    def multiply(k, block):
        target = out_ref if k == INNER - 1 else current
        if block == 0 and k in (0, WITHIN, WITHIN + 1):
            copies[max(k - 1, 0)].wait()
        if k < WITHIN:
            steps = [
                functools.partial(
                    multiply_within, 1 + k, block, part, current, mixed, weights.at[0]
                )
                for part in range(2)
            ]
            return [copies[1 + block].start] + steps if k == 0 else steps
        return [
            functools.partial(
                multiply_part, BOX_BITS[k - WITHIN], SPLITS[k - WITHIN], block, part, target, mixed,
                weights.at[1 + SECOND[k - WITHIN]],
            )
            for part in range(4)
        ]

    def rotate_later(k, block):
        return [] if (k, block) == (0, 1) else rotate(k, block)

    pipeline(INNER, rotate_later, multiply, apart=[(5, 0)])


def inner_levels(*operands):
    return pl.pallas_call(
        inner_kernel,
        in_specs=[VMEM] * 3 + [HBM] * 3,
        out_specs=VMEM,
        out_shape=jax.ShapeDtypeStruct((ROWS, WIDTH), jnp.bfloat16),
        scratch_shapes=[
            pltpu.VMEM((ROWS, WIDTH), jnp.float32),
            pltpu.VMEM((ROWS // 2, 2 * WIDTH), jnp.bfloat16),
            pltpu.VMEM((BOXES, 2 * SLAB, STRIP), jnp.float32),
            pltpu.VMEM((BOXES, 2 * SLAB, STRIP), jnp.float32),
            pltpu.VMEM((3, 2 * WIDTH, 2 * WIDTH), jnp.bfloat16),
            DMA((3,)),
        ],
        compiler_params=pltpu.CompilerParams(vmem_limit_bytes=50 << 20),
        cost_estimate=pl.CostEstimate(flops=9 << 30, bytes_accessed=8 << 20, transcendentals=0),
        name="levels1to9",
    )(*operands)


def outer_kernel(
    data_ref, cos_ref, sin_ref, weight, out_hbm, current, mixed, result, sems
):
    def receive(block):
        rows = slice(block * HALF, (block + 1) * HALF)
        current[rows] = data_ref[rows].astype(jnp.float32)

    leaving = [
        pltpu.make_async_copy(
            result.at[pl.ds(block * HALF, HALF)],
            out_hbm.at[pl.ds(block * HALF, HALF)],
            sems.at[block],
        )
        for block in range(2)
    ]

    def rotate_slabs(k, block, half, i):
        slabs = pair_slabs(k, half, SPLIT, block)[i : i + SLAB]
        first = block * BLOCK + i * SLAB
        at = half * HALF + first
        rotate_into(
            mixed,
            slice(first, first + CHUNK),
            half,
            load_slabs(current, slabs, RE),
            load_slabs(current, slabs, IM),
            cos_ref[k, at : at + CHUNK, :].astype(jnp.float32),
            sin_ref[k, at : at + CHUNK, :].astype(jnp.float32),
        )

    def rotate(k, block):
        arrive = [functools.partial(receive, block)] if k == 0 else []
        return arrive + [
            functools.partial(rotate_slabs, k, block, half, i)
            for half in range(2)
            for i in range(0, BLOCK // SLAB, SLAB)
        ]

    def multiply(k, block):
        target = result if k == 2 else current
        parts = [
            functools.partial(multiply_part, k, SPLIT, block, part, target, mixed, weight)
            for part in range(4)
        ]
        return parts + [leaving[block].start] if k == 2 else parts

    pipeline(3, rotate, multiply)
    for copy in leaving:
        copy.wait()


def outer_levels(*operands):
    return pl.pallas_call(
        outer_kernel,
        in_specs=[VMEM] * len(operands),
        out_specs=HBM,
        out_shape=jax.ShapeDtypeStruct((ROWS, WIDTH), jnp.bfloat16),
        scratch_shapes=[
            pltpu.VMEM((ROWS, WIDTH), jnp.float32),
            pltpu.VMEM((ROWS // 2, 2 * WIDTH), jnp.bfloat16),
            pltpu.VMEM((ROWS, WIDTH), jnp.bfloat16),
            DMA((2,)),
        ],
        compiler_params=pltpu.CompilerParams(vmem_limit_bytes=32 << 20),
        cost_estimate=pl.CostEstimate(flops=3 << 30, bytes_accessed=8 << 20, transcendentals=0),
        name="levels10to12",
    )(*operands)


def exchange(blocks):
    return lax.all_to_all(blocks, AXES, 0, 0, tiled=True)


def on_device(signal, box_phase, node_phase, local_interp, across_x, across_y):
    own = box_phase[:, 0]
    moved = exchange(first_levels(signal[0, 0], own, node_phase, local_interp))
    last_cos, last_sin, own_cos, own_sin, local, *weights = prep(
        own, node_phase, local_interp, across_x, across_y
    )
    inner = inner_levels(moved, own_cos, own_sin, *weights)
    return outer_levels(exchange(inner), last_cos, last_sin, local)[None, None]


def solution(mesh):
    return jax.shard_map(
        on_device,
        mesh=mesh,
        in_specs=(P("sx", "sy", None, None), P(None, "sx", "sy", None), P(), P(), P(), P()),
        out_specs=P("sx", "sy", None, None),
        check_vma=False,
    )
```

```python
import functools

import jax
import jax.numpy as jnp
from jax import lax
from jax.experimental import pallas as pl
from jax.experimental.pallas import tpu as pltpu
from jax.sharding import PartitionSpec as P

AXES = ("sx", "sy")
ROWS = 1024
NODES = 256
WIDTH = 512
BOXES = 128
SLAB = 8
CHUNK = 64
HALF = ROWS // 2
STRIP = 128
CODE = 38.0
MESSAGE = 48
DATA = 32
FIRST = 1
INNER = 9
LAST = FIRST + INNER
WITHIN = 2
BLOCK = 256
BOX_BITS = (4, 0, 5, 1, 6, 2, 3)
SECOND = (0, 1, 0, 1, 0, 1, 1)
SPLITS = (6, 6, 6, 5, 5, 5, 5)
SPLIT = 6

SIN = (9.99999242e-01, -1.66656797e-01, 8.31322541e-03, -1.85234428e-04)
COS = (0.99999325, -0.49991211, 0.04148738, -0.00127111)


def horner(coefficients, x):
    total = coefficients[-1] * x + coefficients[-2]
    for factor in coefficients[-3::-1]:
        total = total * x + factor
    return total


def cos_sin(angle):
    half = angle * 0.5
    square = half * half
    sine = half * horner(SIN, square)
    cosine = horner(COS, square)
    double = sine + sine
    return 1.0 - double * sine, double * cosine


def pair_slabs(bit, half, split, block):
    return [
        slab
        for slab in range(BOXES)
        if slab >> bit & 1 == half and slab >> split & 1 == block
    ]


def runs(slabs):
    found = []
    for i, slab in enumerate(slabs):
        if found and found[-1][1] + found[-1][2] == slab * SLAB:
            found[-1][2] += SLAB
        else:
            found.append([i * SLAB, slab * SLAB, SLAB])
    return found


def load_slabs(ref, slabs, columns):
    parts = [ref[r : r + n, columns] for _, r, n in runs(slabs)]
    return parts[0] if len(parts) == 1 else jnp.concatenate(parts, axis=0)


def interleave(major, minor):
    done = 0
    for i, step in enumerate(major):
        step()
        upto = len(minor) * (i + 1) // len(major)
        for other in minor[done:upto]:
            other()
        done = upto
    for other in minor[done:]:
        other()


def pipeline(levels, rotate, multiply, apart=()):
    stages = [(k, block) for k in range(levels) for block in range(2)]
    ready = rotate(*stages[0])
    for i, stage in enumerate(stages):
        if i == 0 or stage in apart:
            interleave(ready, [])
        after = stages[i + 1] if i + 1 < len(stages) else None
        ready = rotate(*after) if after else []
        interleave(multiply(*stage), [] if after in apart else ready)


RE = slice(0, NODES)
IM = slice(NODES, WIDTH)


VMEM = pl.BlockSpec(memory_space=pltpu.VMEM)
HBM = pl.BlockSpec(memory_space=pltpu.HBM)
DMA = pltpu.SemaphoreType.DMA


def fill_weight(weight, interp):
    for child in range(2):
        for source in range(2):
            rows = slice(source * NODES, (source + 1) * NODES)
            columns = slice(child * NODES, (child + 1) * NODES)
            real = interp[child, source, 0].astype(jnp.float32)
            imag = interp[child, source, 1].astype(jnp.float32)
            for i, factor in enumerate((real, imag - real, imag + real)):
                weight[i, rows, columns] = factor.astype(jnp.bfloat16)


def product(mixed, block, child, weight):
    rows = slice(block * BLOCK, (block + 1) * BLOCK)
    both, real, imag = [
        jnp.dot(
            mixed[rows, i * WIDTH : (i + 1) * WIDTH],
            weight[i, :, child * NODES : (child + 1) * NODES],
            preferred_element_type=jnp.float32,
        )
        for i in range(3)
    ]
    return jnp.concatenate([both - imag, both + real], axis=1)


def keep(mixed, rows, half, column, re, im):
    for i, values in enumerate((re + im, re, im)):
        first = i * WIDTH + half * NODES + column
        mixed[rows, first : first + values.shape[-1]] = values.astype(jnp.bfloat16)


def strip(j):
    return slice(j * STRIP, (j + 1) * STRIP)


def rotate_into(mixed, rows, half, re, im, c, s):
    keep(mixed, rows, half, 0, re * c - im * s, re * s + im * c)


def swap(bit, zero, one):
    distance = 1 << bit
    at_zero = lax.broadcasted_iota(jnp.int32, zero.shape, 1) & distance == 0
    return (
        jnp.where(at_zero, zero, pltpu.roll(one, distance, 1)),
        jnp.where(at_zero, pltpu.roll(zero, SLAB - distance, 1), one),
    )


def mix_within(bit, block, i, j, sides, mixed):
    at = block * BLOCK + i * CHUNK
    swapped = [
        swap(bit, *[side[part].reshape(CHUNK // SLAB, SLAB, STRIP) for side in sides])
        for part in range(2)
    ]
    for half in range(2):
        re, im = [swapped[part][half].reshape(CHUNK, STRIP) for part in range(2)]
        keep(mixed, slice(at, at + CHUNK), half, j * STRIP, re, im)


def multiply_within(bit, block, target, mixed, weight):
    pair = [
        product(mixed, block, child, weight).reshape(BLOCK // SLAB, SLAB, WIDTH)
        for child in range(2)
    ]
    for side, rows in enumerate(swap(bit, *pair)):
        first = block * HALF + side * BLOCK
        target[first : first + BLOCK] = rows.reshape(BLOCK, WIDTH)


def first_kernel(
    data_hbm, box_ref, node_hbm, interp_hbm, out_hbm,
    data, nodes, interp, weight, cosines, sines, current, mixed, messages, sems,
):
    halves = [pl.ds(block * HALF, HALF) for block in range(2)]
    node_copies = [
        pltpu.make_async_copy(node_hbm.at[0, half], nodes.at[half], sems.at[block])
        for block, half in enumerate(halves)
    ]
    data_copies = [
        pltpu.make_async_copy(data_hbm.at[half], data.at[half], sems.at[2 + block])
        for block, half in enumerate(halves)
    ]
    interp_copy = pltpu.make_async_copy(interp_hbm, interp, sems.at[4])
    node_copies[0].start()
    interp_copy.start()
    data_copies[0].start()
    node_copies[1].start()
    data_copies[1].start()
    box_cos, box_sin = cos_sin(box_ref[0])
    next_cos, next_sin = cos_sin(box_ref[1])
    phases = [box_ref[FIRST + 1 + k][:, strip(j)] for j in range(2) for k in range(SLAB)]
    code = jnp.exp2(jnp.concatenate(phases, axis=0) * CODE).astype(jnp.bfloat16)
    messages[:, DATA:, :] = jnp.broadcast_to(code[None], (BOXES, 2 * SLAB, STRIP))

    def form(first, j):
        rows, columns = slice(first, first + CHUNK), strip(j)
        node_cos, node_sin = cos_sin(nodes[rows, columns])
        c, s = box_cos[:, columns], box_sin[:, columns]
        cosines[rows, columns] = node_cos * c - node_sin * s
        sines[rows, columns] = node_sin * c + node_cos * s

    node_copies[0].wait()
    for first in range(0, HALF, CHUNK):
        for j in range(2):
            form(first, j)
    interp_copy.wait()
    fill_weight(weight, interp)

    def rotate_rows(block, i, j):
        sides = []
        for side in range(2):
            first = block * HALF + side * BLOCK + i * CHUNK
            rows = slice(first, first + CHUNK)
            c, s = cosines[rows, strip(j)], sines[rows, strip(j)]
            re = data[rows, strip(j)].astype(jnp.float32)
            im = data[rows, strip(2 + j)].astype(jnp.float32)
            sides.append((re * c - im * s, re * s + im * c))
        mix_within(0, block, i, j, sides, mixed)

    def rotate(k, block):
        data_copies[block].wait()
        steps = [
            functools.partial(rotate_rows, block, i, j)
            for i in range(BLOCK // CHUNK)
            for j in range(2)
        ]
        if block == 0:
            return steps
        node_copies[1].wait()
        forms = [
            functools.partial(form, first, j)
            for first in range(HALF, ROWS, CHUNK)
            for j in range(2)
        ]
        return forms + steps

    def pack(block, i):
        first = block * HALF + i * CHUNK
        rows, slabs = slice(first, first + CHUNK), slice(first // SLAB, (first + CHUNK) // SLAB)
        turned = []
        for j in range(2):
            c, s = next_cos[:, strip(j)], next_sin[:, strip(j)]
            re, im = current[rows, strip(j)], current[rows, strip(2 + j)]
            turned.append((re * c - im * s, re * s + im * c))
        for part in range(2):
            pair = [turned[j][part].reshape(CHUNK // SLAB, SLAB, STRIP) for j in range(2)]
            messages[slabs, 2 * SLAB * part : 2 * SLAB * (part + 1), :] = jnp.concatenate(
                pair, axis=1
            ).astype(jnp.bfloat16)

    batch = 2 * CHUNK // SLAB
    leaving = [
        pltpu.make_async_copy(
            messages.at[pl.ds(first, batch)], out_hbm.at[pl.ds(first, batch)], sems.at[5 + i]
        )
        for i, first in enumerate(range(0, BOXES, batch))
    ]

    def multiply(k, block):
        steps = [
            functools.partial(multiply_within, 0, block, current, mixed, weight)
        ]
        for i in range(HALF // CHUNK):
            steps.append(functools.partial(pack, block, i))
            if i % 2:
                steps.append(leaving[(block * (HALF // CHUNK) + i) // 2].start)
        return steps

    pipeline(1, rotate, multiply)
    for copy in leaving:
        copy.wait()


def first_levels(data, box_phase, node_phase, interp):
    return pl.pallas_call(
        first_kernel,
        in_specs=[HBM, VMEM, HBM, HBM],
        out_specs=HBM,
        out_shape=jax.ShapeDtypeStruct((BOXES, MESSAGE, STRIP), jnp.bfloat16),
        scratch_shapes=[
            pltpu.VMEM((ROWS, WIDTH), jnp.bfloat16),
            pltpu.VMEM((ROWS, NODES), jnp.float32),
            pltpu.VMEM((2, 2, 2, NODES, NODES), jnp.bfloat16),
            pltpu.VMEM((3, WIDTH, WIDTH), jnp.bfloat16),
            pltpu.VMEM((ROWS, NODES), jnp.float32),
            pltpu.VMEM((ROWS, NODES), jnp.float32),
            pltpu.VMEM((ROWS, WIDTH), jnp.float32),
            pltpu.VMEM((ROWS // 2, 3 * WIDTH), jnp.bfloat16),
            pltpu.VMEM((BOXES, MESSAGE, STRIP), jnp.bfloat16),
            DMA((13,)),
        ],
        compiler_params=pltpu.CompilerParams(vmem_limit_bytes=58 << 20),
        cost_estimate=pl.CostEstimate(flops=1 << 30, bytes_accessed=8 << 20, transcendentals=0),
        name="level0",
    )(data, box_phase, node_phase, interp)


def prep_kernel(
    box_ref, node_hbm, local_hbm, x_hbm, y_hbm,
    cos_ref, sin_ref, own_cos, own_sin, local_weight, inner_weights,
    own, nodes, interps, sems,
):
    me = lax.axis_index("sx") * lax.axis_size("sy") + lax.axis_index("sy")
    rows = pl.ds(pl.multiple_of(me * SLAB, SLAB), SLAB)
    copies = [
        pltpu.make_async_copy(node_hbm.at[pl.ds(FIRST, INNER), rows, :], own, sems.at[0]),
    ] + [pltpu.make_async_copy(node_hbm.at[LAST + k], nodes.at[k], sems.at[1 + k]) for k in range(3)]
    copies += [
        pltpu.make_async_copy(hbm, interps.at[k], sems.at[4 + k])
        for k, hbm in enumerate((x_hbm, y_hbm, local_hbm))
    ]
    for copy in copies:
        copy.start()
    copies[0].wait()
    own_cos[...], own_sin[...] = cos_sin(own[...])
    for k in range(3):
        copies[4 + k].wait()
        fill_weight(inner_weights.at[(k + 1) % 3], interps.at[k])
    fill_weight(local_weight, interps.at[2])
    for k in range(3):
        copies[1 + k].wait()
        box_cos, box_sin = cos_sin(box_ref[LAST + k])
        for half in range(2):
            for block in range(2):
                slabs = pair_slabs(k, half, SPLIT, block)
                for i in range(0, len(slabs), SLAB):
                    angles = load_slabs(nodes.at[k], slabs[i : i + SLAB], slice(None))
                    node_cos, node_sin = cos_sin(angles)
                    at = half * HALF + block * BLOCK + i * SLAB
                    cosine = node_cos * box_cos - node_sin * box_sin
                    sine = node_sin * box_cos + node_cos * box_sin
                    cos_ref[k, at : at + CHUNK, :] = cosine.astype(jnp.bfloat16)
                    sin_ref[k, at : at + CHUNK, :] = sine.astype(jnp.bfloat16)


def prep(box_phase, node_phase, *interps):
    weight = jax.ShapeDtypeStruct((3, WIDTH, WIDTH), jnp.bfloat16)
    weights = jax.ShapeDtypeStruct((3, 3, WIDTH, WIDTH), jnp.bfloat16)
    table = jax.ShapeDtypeStruct((3, ROWS, NODES), jnp.bfloat16)
    own = jax.ShapeDtypeStruct((INNER, SLAB, NODES), jnp.float32)
    return pl.pallas_call(
        prep_kernel,
        in_specs=[VMEM] + [HBM] * 4,
        out_specs=[VMEM] * 6,
        out_shape=[table, table, own, own, weight, weights],
        scratch_shapes=[
            pltpu.VMEM((INNER, SLAB, NODES), jnp.float32),
            pltpu.VMEM((3, ROWS, NODES), jnp.float32),
            pltpu.VMEM((3, 2, 2, 2, NODES, NODES), jnp.bfloat16),
            DMA((7,)),
        ],
        compiler_params=pltpu.CompilerParams(vmem_limit_bytes=52 << 20),
        cost_estimate=pl.CostEstimate(flops=60_000_000, bytes_accessed=7 << 20, transcendentals=0),
        name="prep",
    )(box_phase, node_phase, *interps)


def multiply_child(bit, split, block, child, target, mixed, weight):
    total = product(mixed, block, child, weight)
    for at, r, n in runs(pair_slabs(bit, child, split, block)):
        target[r : r + n] = total[at : at + n].astype(target.dtype)


def inner_kernel(
    data_ref, own_cos, own_sin, weights_hbm, out_ref,
    current, mixed, box_cos, box_sin, weights, sems,
):
    copies = [
        pltpu.make_async_copy(weights_hbm.at[i], weights.at[i], sems.at[i]) for i in range(3)
    ]
    copies[0].start()

    def receive(block, part):
        boxes = slice(block * CHUNK, (block + 1) * CHUNK)
        if part == 2:
            phase = jnp.log2(data_ref[boxes, DATA:, :].astype(jnp.float32)) * (1.0 / CODE)
            box_cos[boxes], box_sin[boxes] = cos_sin(phase)
        else:
            pair = data_ref[boxes, 2 * SLAB * part : 2 * SLAB * (part + 1), :].astype(jnp.float32)
            for i in range(2):
                piece = pair[:, i * SLAB : (i + 1) * SLAB, :]
                current[block * HALF : (block + 1) * HALF, strip(2 * part + i)] = piece.reshape(
                    HALF, STRIP
                )

    def turn(k, j, slabs):
        node_cos, node_sin = own_cos[k, :, strip(j)], own_sin[k, :, strip(j)]
        at = slice(SLAB * j + k - 1, SLAB * j + k)
        re_parts, im_parts = [], []
        for slab in slabs:
            if k:
                c, s = box_cos[slab, at, :], box_sin[slab, at, :]
                cosine = c * node_cos - s * node_sin
                sine = s * node_cos + c * node_sin
            else:
                cosine, sine = node_cos, node_sin
            rows = slice(slab * SLAB, (slab + 1) * SLAB)
            re, im = current[rows, strip(j)], current[rows, strip(2 + j)]
            re_parts.append(re * cosine - im * sine)
            im_parts.append(re * sine + im * cosine)
        return jnp.concatenate(re_parts, axis=0), jnp.concatenate(im_parts, axis=0)

    def rotate_within(k, block, i, j):
        first = (block * HALF + i * CHUNK) // SLAB
        sides = [
            turn(k, j, range(first + side, first + side + SLAB)) for side in (0, BLOCK // SLAB)
        ]
        mix_within(1 + k, block, i, j, sides, mixed)

    def rotate_slabs(k, block, half, i, j):
        slabs = pair_slabs(BOX_BITS[k - WITHIN], half, SPLITS[k - WITHIN], block)[i : i + SLAB]
        first = block * BLOCK + i * SLAB
        to = slice(first, first + CHUNK)
        keep(mixed, to, half, j * STRIP, *turn(k, j, slabs))

    def rotate(k, block):
        if k >= WITHIN:
            return [
                functools.partial(rotate_slabs, k, block, half, i, j)
                for half in range(2)
                for i in range(0, BLOCK // SLAB, SLAB)
                for j in range(2)
            ]
        steps = [
            functools.partial(rotate_within, k, block, i, j)
            for i in range(BLOCK // CHUNK)
            for j in range(2)
        ]
        if k:
            return steps
        steps = [functools.partial(receive, block, part) for part in range(3)] + steps
        return steps + rotate(0, 1) if block == 0 else steps

    def multiply(k, block):
        target = out_ref if k == INNER - 1 else current
        if block == 0 and k in (0, WITHIN, WITHIN + 1):
            copies[max(k - 1, 0)].wait()
        if k < WITHIN:
            steps = [
                functools.partial(
                    multiply_within, 1 + k, block, current, mixed, weights.at[0]
                )
            ]
            return [copies[1 + block].start] + steps if k == 0 else steps
        return [
            functools.partial(
                multiply_child, BOX_BITS[k - WITHIN], SPLITS[k - WITHIN], block, child, target,
                mixed, weights.at[1 + SECOND[k - WITHIN]],
            )
            for child in range(2)
        ]

    def rotate_later(k, block):
        return [] if (k, block) == (0, 1) else rotate(k, block)

    pipeline(INNER, rotate_later, multiply, apart=[(5, 0)])


def inner_levels(*operands):
    return pl.pallas_call(
        inner_kernel,
        in_specs=[VMEM] * 3 + [HBM],
        out_specs=VMEM,
        out_shape=jax.ShapeDtypeStruct((ROWS, WIDTH), jnp.bfloat16),
        scratch_shapes=[
            pltpu.VMEM((ROWS, WIDTH), jnp.float32),
            pltpu.VMEM((ROWS // 2, 3 * WIDTH), jnp.bfloat16),
            pltpu.VMEM((BOXES, 2 * SLAB, STRIP), jnp.float32),
            pltpu.VMEM((BOXES, 2 * SLAB, STRIP), jnp.float32),
            pltpu.VMEM((3, 3, WIDTH, WIDTH), jnp.bfloat16),
            DMA((3,)),
        ],
        compiler_params=pltpu.CompilerParams(vmem_limit_bytes=50 << 20),
        cost_estimate=pl.CostEstimate(flops=9 << 30, bytes_accessed=8 << 20, transcendentals=0),
        name="levels1to9",
    )(*operands)


def outer_kernel(
    data_ref, cos_ref, sin_ref, weight, out_hbm, current, mixed, result, sems
):
    def receive(block):
        rows = slice(block * HALF, (block + 1) * HALF)
        current[rows] = data_ref[rows].astype(jnp.float32)

    leaving = [
        pltpu.make_async_copy(
            result.at[pl.ds(block * HALF, HALF)],
            out_hbm.at[pl.ds(block * HALF, HALF)],
            sems.at[block],
        )
        for block in range(2)
    ]

    def rotate_slabs(k, block, half, i):
        slabs = pair_slabs(k, half, SPLIT, block)[i : i + SLAB]
        first = block * BLOCK + i * SLAB
        at = half * HALF + first
        rotate_into(
            mixed,
            slice(first, first + CHUNK),
            half,
            load_slabs(current, slabs, RE),
            load_slabs(current, slabs, IM),
            cos_ref[k, at : at + CHUNK, :].astype(jnp.float32),
            sin_ref[k, at : at + CHUNK, :].astype(jnp.float32),
        )

    def rotate(k, block):
        arrive = [functools.partial(receive, block)] if k == 0 else []
        return arrive + [
            functools.partial(rotate_slabs, k, block, half, i)
            for half in range(2)
            for i in range(0, BLOCK // SLAB, SLAB)
        ]

    def multiply(k, block):
        target = result if k == 2 else current
        parts = [
            functools.partial(multiply_child, k, SPLIT, block, child, target, mixed, weight)
            for child in range(2)
        ]
        return parts + [leaving[block].start] if k == 2 else parts

    pipeline(3, rotate, multiply)
    for copy in leaving:
        copy.wait()


def outer_levels(*operands):
    return pl.pallas_call(
        outer_kernel,
        in_specs=[VMEM] * len(operands),
        out_specs=HBM,
        out_shape=jax.ShapeDtypeStruct((ROWS, WIDTH), jnp.bfloat16),
        scratch_shapes=[
            pltpu.VMEM((ROWS, WIDTH), jnp.float32),
            pltpu.VMEM((ROWS // 2, 3 * WIDTH), jnp.bfloat16),
            pltpu.VMEM((ROWS, WIDTH), jnp.bfloat16),
            DMA((2,)),
        ],
        compiler_params=pltpu.CompilerParams(vmem_limit_bytes=32 << 20),
        cost_estimate=pl.CostEstimate(flops=3 << 30, bytes_accessed=8 << 20, transcendentals=0),
        name="levels10to12",
    )(*operands)


def exchange(blocks):
    return lax.all_to_all(blocks, AXES, 0, 0, tiled=True)


def on_device(signal, box_phase, node_phase, local_interp, across_x, across_y):
    own = box_phase[:, 0]
    moved = exchange(first_levels(signal[0, 0], own, node_phase, local_interp))
    last_cos, last_sin, own_cos, own_sin, local, weights = prep(
        own, node_phase, local_interp, across_x, across_y
    )
    inner = inner_levels(moved, own_cos, own_sin, weights)
    return outer_levels(exchange(inner), last_cos, last_sin, local)[None, None]


def solution(mesh):
    return jax.shard_map(
        on_device,
        mesh=mesh,
        in_specs=(P("sx", "sy", None, None), P(None, "sx", "sy", None), P(), P(), P(), P()),
        out_specs=P("sx", "sy", None, None),
        check_vma=False,
    )
```
